128 devices in a mesh: row: 4 (over y), col: 8 (over z, core), depth: 4 (over x).
Axes of the slice: x: 4, y: 4, z: 4, core: 2. Of those that a mesh axis runs over, the one named last changes fastest.
Arguments:
- stacked_signals: bfloat16 [1024, 512, 256], P('depth', ('row', 'col')), may hold values from -6 to 6
- presence_indicator: bfloat16 [1024, 512], P('depth', ('row', 'col')), may hold values from 0 to 1, as said below
- normalizer_multiplier: float32 [256], replicated, may hold values from 0.5 to 1.5
- normalizer_shift: float32 [256], replicated, may hold values from -3 to 3
- leading_linear_map: bfloat16 [256, 32], replicated, may hold values from -0.375 to 0.375
- first_projection_offset: float32 [32], replicated, may hold values from -3 to 3
- trailing_linear_map: bfloat16 [256, 32], replicated, may hold values from -0.375 to 0.375
- second_projection_offset: float32 [32], replicated, may hold values from -3 to 3
- final_projection_matrix: bfloat16 [1024, 128], replicated, may hold values from -0.1875 to 0.1875
Outputs:
- pair_update: bfloat16 [512, 512, 128], P(('row', 'depth'), 'col')
The draws below stay inside these ranges and needn't reach their ends.
Inputs may be any that keep to these rules, and one draw needn't show every extreme that they name: `presence_indicator`: 0 marks a residue absent from a sequence; some residues are absent from every sequence.
All inputs are finite; a program needn't handle non-finite values.
Results may differ from the reference program's by a relative error of at most 0.0036.
Values may be sent and summed in bfloat16 or wider, within the bound.
No kernel may reach another device: no remote copies, remote signals or barrier semaphores. Data moves between devices by JAX's collectives and lax.ppermute only.
A program may use at most 64 MiB of HBM per device.

```python
import math
import jax
import jax.numpy as jnp
from jax import lax

INPUT_DIMS = 256
HIDDEN_SIZE = 32
CZ = 128
SEQ_DEV = 256
RELATIVE_TALLY = 1024
AMINO_TALLY = 512
N_DEPTH = 4


def draw_presence_indicator(key, part):
    key = jax.random.fold_in(key, 7)
    key_res, key_start, key_len, key_wt = jax.random.split(key, 4)
    present = (jax.random.randint(key_res, (AMINO_TALLY,), 0, 16) != 0).astype(jnp.float32)
    start = jax.random.randint(key_start, (RELATIVE_TALLY, 1), -(AMINO_TALLY // 2), AMINO_TALLY // 2 + 1)
    length = jax.random.randint(key_len, (RELATIVE_TALLY, 1), AMINO_TALLY // 2, 3 * AMINO_TALLY // 2 + 1)
    position = jnp.arange(AMINO_TALLY, dtype=jnp.int32)[None, :]
    cover = ((position >= start) & (position < start + length)).astype(jnp.float32)
    weight = jax.random.uniform(key_wt, (RELATIVE_TALLY, AMINO_TALLY), jnp.float32, 0.05, 1.0)
    return (cover * weight * present[None, :]).astype(jnp.bfloat16)


def level_of(stream_key, shape, cuts, smallest, largest):
    gain, own = 1.0, jax.random.fold_in(stream_key, 6)
    for dim, blocks in cuts:
        heights = jnp.exp(jax.random.uniform(jax.random.fold_in(own, dim), (blocks,), jnp.float32, smallest / len(cuts), largest / len(cuts)))
        gain = gain * jnp.repeat(heights, shape[dim] // blocks).reshape([-1 if axis == dim else 1 for axis in range(len(shape))])
    return gain


def scatter_about(key, dims, scale, bound, pieces=(), kind=jnp.bfloat16):
    entries = jax.random.normal(key, dims, jnp.float32) * scale
    if len(pieces) > 0:
        entries = level_of(key, dims, pieces, -0.22, 0.18) * entries
    return jnp.clip(entries, min=-bound, max=bound).astype(kind)


def setup_inputs(seed: int = 0) -> dict:
    arg_keys = jax.random.split(jax.random.key(seed), 10)
    return {
        "stacked_signals": scatter_about(arg_keys[0], (RELATIVE_TALLY, AMINO_TALLY, INPUT_DIMS), 1.0, 6.0, ((0, 4), (1, 32))),
        "presence_indicator": draw_presence_indicator(jax.random.fold_in(arg_keys[9], 71), 0),
        "normalizer_multiplier": jnp.clip(1.0 + 0.1 * jax.random.normal(arg_keys[2], (INPUT_DIMS,), jnp.float32), 0.5, 1.5),
        "normalizer_shift": scatter_about(arg_keys[3], (INPUT_DIMS,), 0.5, 3.0, (), jnp.float32),
        "leading_linear_map": scatter_about(arg_keys[4], (INPUT_DIMS, HIDDEN_SIZE), INPUT_DIMS ** -0.5, 0.375),
        "first_projection_offset": scatter_about(arg_keys[5], (HIDDEN_SIZE,), 0.5, 3.0, (), jnp.float32),
        "trailing_linear_map": scatter_about(arg_keys[6], (INPUT_DIMS, HIDDEN_SIZE), INPUT_DIMS ** -0.5, 0.375),
        "second_projection_offset": scatter_about(arg_keys[7], (HIDDEN_SIZE,), 0.5, 3.0, (), jnp.float32),
        "final_projection_matrix": scatter_about(arg_keys[8], (HIDDEN_SIZE * HIDDEN_SIZE, CZ), (HIDDEN_SIZE * HIDDEN_SIZE) ** -0.5, 0.1875),
    }


def project(normed, weight, bias, mask_floating):
    homolog_lines, residues, feature_depth = normed.shape
    flat = jnp.dot(normed.reshape(homolog_lines * residues, feature_depth), weight, preferred_element_type=jnp.float32)
    flat = flat + bias
    return (flat.reshape(homolog_lines, residues, -1) * mask_floating[:, :, None]).astype(jnp.bfloat16)

def reference(stacked_signals, presence_indicator, normalizer_multiplier, normalizer_shift, leading_linear_map, first_projection_offset, trailing_linear_map, second_projection_offset, final_projection_matrix):
    mask_floating = presence_indicator.astype(jnp.float32)
    element_count = stacked_signals.astype(jnp.float32)
    center = element_count - lax.optimization_barrier(jnp.mean(element_count, axis=-1, keepdims=True))
    spread = lax.optimization_barrier(jnp.mean(center * center, axis=-1, keepdims=True))
    normed = (center * lax.rsqrt(spread + 1e-05) * normalizer_multiplier + normalizer_shift).astype(jnp.bfloat16)
    left = project(normed, leading_linear_map, first_projection_offset, mask_floating)
    right = project(normed, trailing_linear_map, second_projection_offset, mask_floating)
    count = jnp.dot(mask_floating.T, mask_floating, precision=lax.Precision.HIGHEST)
    weight3 = final_projection_matrix.astype(jnp.float32).reshape(HIDDEN_SIZE, HIDDEN_SIZE, CZ)
    residues = left.shape[1]
    block = math.gcd(residues, 64)
    nblocks = residues // block
    left_blocks = jnp.moveaxis(left.reshape(RELATIVE_TALLY, nblocks, block, HIDDEN_SIZE), 1, 0)
    count_blocks = count.reshape(nblocks, block, residues)

    def one_block(pair):
        lblock, cblock = pair
        total = jnp.zeros((block, residues, CZ), jnp.float32)
        for group in range(N_DEPTH):
            lpart = lblock[group * SEQ_DEV:(group + 1) * SEQ_DEV].astype(jnp.float32)
            rpart = right[group * SEQ_DEV:(group + 1) * SEQ_DEV].astype(jnp.float32)
            outer = jnp.einsum('sic,sjd->icjd', lpart, rpart).astype(jnp.bfloat16)
            total = total + jnp.einsum('icjd,cde->ije', outer.astype(jnp.float32), weight3)
        return (total / jnp.maximum(cblock, 1.0)[:, :, None]).astype(jnp.bfloat16)
    result = lax.map(one_block, (left_blocks, count_blocks))
    return result.reshape(residues, residues, CZ)
```

```python
import functools

import jax
import jax.numpy as jnp
from jax import lax
from jax.experimental import pallas as pl
from jax.experimental.pallas import tpu as pltpu
from jax.sharding import PartitionSpec as P

F32 = jnp.float32
BF16 = jnp.bfloat16
NT = (((1,), (1,)), ((), ()))
NN = (((1,), (0,)), ((), ()))

SEQ = 256
RES = 16
HID = 32
SHARD = RES * HID
ROWS = SHARD + RES


def dot(a, b, dims):
    return lax.dot_general(a, b, dims, preferred_element_type=F32)


def project_kernel(sig, mask, gain, shift, w_left, b_left, w_right, b_right, left, right, wide, cols, turn):
    half = sig.shape[0]

    @pl.when(pl.program_id(0) == 0)
    def _():
        turn[...] = jnp.zeros_like(turn)
        turn[0:256, 0:HID] = w_left[...].astype(F32)
        turn[0:256, HID : 2 * HID] = w_right[...].astype(F32)
        turn[256:384, 0:HID] = jnp.broadcast_to(b_left[...], (128, HID))
        turn[256:384, HID : 2 * HID] = jnp.broadcast_to(b_right[...], (128, HID))

    weights = jnp.transpose(turn[0:256, :])[0 : 2 * HID, :].astype(BF16)
    bias = jnp.transpose(turn[256:384, :])[0 : 2 * HID, :]
    turn[384 : 384 + half, 0:RES] = mask[...].astype(F32)
    presence = jnp.transpose(turn[384 : 384 + half, :])[0:RES, :]

    flat = sig[...].astype(F32).reshape(half * RES, 256)
    wide[0] = flat[:, 0:128]
    wide[1] = flat[:, 128:256]
    for r in range(RES):
        low = wide[0, pl.ds(r, half, stride=RES), :]
        high = wide[1, pl.ds(r, half, stride=RES), :]
        mean = jnp.sum(low + high, axis=1, keepdims=True) * (1.0 / 256)
        low = low - mean
        high = high - mean
        spread = jnp.sum(low * low + high * high, axis=1, keepdims=True) * (1.0 / 256)
        scale = lax.rsqrt(spread + 1e-5)
        low = low * scale * gain[:, 0:128] + shift[:, 0:128]
        high = high * scale * gain[:, 128:256] + shift[:, 128:256]
        normed = jnp.concatenate([low.astype(BF16), high.astype(BF16)], axis=1)
        both = (dot(weights, normed, NT) + bias) * presence[r : r + 1, :]
        left[r * HID : (r + 1) * HID, :] = both[0:HID].astype(BF16)
        cols[r * HID : (r + 1) * HID, :] = both[HID : 2 * HID]
    for d in range(HID):
        right[d * RES : (d + 1) * RES, :] = cols[pl.ds(d, RES, stride=HID), :].astype(BF16)
    left[SHARD:ROWS, :] = presence.astype(BF16)
    right[SHARD:ROWS, :] = presence.astype(BF16)


def project(sig, mask, gain, shift, w_left, b_left, w_right, b_right):
    steps = 2
    half = SEQ // steps
    whole = lambda shape: pl.BlockSpec(shape, lambda s: (0,) * len(shape))
    return pl.pallas_call(
        project_kernel,
        grid=(steps,),
        in_specs=[
            pl.BlockSpec((half, RES, 256), lambda s: (s, 0, 0)),
            pl.BlockSpec((half, RES), lambda s: (s, 0)),
            whole((1, 256)),
            whole((1, 256)),
            whole((256, HID)),
            whole((1, HID)),
            whole((256, HID)),
            whole((1, HID)),
        ],
        out_specs=[pl.BlockSpec((ROWS, half), lambda s: (0, s))] * 2,
        out_shape=[jax.ShapeDtypeStruct((ROWS, SEQ), BF16)] * 2,
        scratch_shapes=[
            pltpu.VMEM((2, half * RES, 128), F32),
            pltpu.VMEM((SHARD, half), F32),
            pltpu.VMEM((384 + half, 128), F32),
        ],
        compiler_params=pltpu.CompilerParams(vmem_limit_bytes=40 * 2**20),
        name="project",
    )(sig, mask, gain, shift, w_left, b_left, w_right, b_right)


def pair_kernel(own, place, *refs):
    lefts, rights, mix = refs[0:4], refs[4:12], refs[12]
    if own:
        out, count, outer, chosen = refs[13:]
    else:
        out, outer, chosen = refs[13:]
    which = place[0]
    for t in range(4):

        @pl.when(which == t)
        def _():
            chosen[...] = lefts[t][...]

    @pl.loop(0, HID // 2)
    def _(step):
        parts = []
        for dd in range(2):
            start = pl.multiple_of(step * 2 * RES + dd * RES, RES)
            for ref in rights:
                parts.append(ref[pl.ds(start, RES), :])
        block = jnp.concatenate(parts, axis=0)
        prod = dot(chosen[0:SHARD, :], block, NT).astype(BF16)
        for dd in range(2):
            at = pl.multiple_of(step * 2 * HID + dd * HID, HID)
            for i in range(RES):
                outer[i // 2, pl.ds(at, HID), (i % 2) * 128 : (i % 2) * 128 + 128] = prod[
                    i * HID : (i + 1) * HID, dd * 128 : (dd + 1) * 128
                ]

    @pl.loop(0, RES // 2)
    def _(pair):
        mixed = dot(mix[...], outer[pair], NN)
        for ii in range(2):
            out[pair * 2 + ii] = jnp.transpose(mixed[:, ii * 128 : (ii + 1) * 128]).astype(out.dtype)

    weights = jnp.concatenate([ref[SHARD:ROWS, :] for ref in rights], axis=0)
    tally = jnp.concatenate([chosen[SHARD:ROWS, :], jnp.zeros((128 - RES, SEQ), BF16)], axis=0)
    tally = dot(weights, tally, NT)
    if own:
        count[...] = tally
    else:
        high = tally.astype(BF16)
        out[RES] = high
        out[RES + 1] = (tally - high.astype(F32)).astype(BF16)


def pair(own, place, lefts, rights, mix):
    vmem = pl.BlockSpec(memory_space=pltpu.VMEM)
    if own:
        out_shape = [
            jax.ShapeDtypeStruct((RES, 128, 128), F32),
            jax.ShapeDtypeStruct((128, 128), F32),
        ]
    else:
        out_shape = [jax.ShapeDtypeStruct((RES + 2, 128, 128), BF16)]
    return pl.pallas_call(
        functools.partial(pair_kernel, own),
        in_specs=[pl.BlockSpec(memory_space=pltpu.SMEM)] + [vmem] * 13,
        out_specs=[vmem] * len(out_shape),
        out_shape=out_shape,
        scratch_shapes=[
            pltpu.VMEM((RES // 2, HID * HID, 256), BF16),
            pltpu.VMEM((ROWS, SEQ), BF16),
        ],
        compiler_params=pltpu.CompilerParams(vmem_limit_bytes=40 * 2**20),
        cost_estimate=pl.CostEstimate(
            flops=2 * SHARD * SHARD * 8 * SEQ + 2 * 128 * 16 * 128 * 1024,
            bytes_accessed=5 * 2**20,
            transcendentals=0,
        ),
        name="pair",
    )(place, *lefts, *rights, mix)


def settle_kernel(place, mine, count, a, b, c, *refs):
    pieces, inverse = refs[0:4], refs[4]
    total = count[...]
    for ref in (a, b, c):
        total = total + (ref[RES].astype(F32) + ref[RES + 1].astype(F32))
    inverse[...] = 1.0 / jnp.maximum(total, 1.0)
    for u in range(4):
        for h in range(2):
            start = pl.multiple_of(place[u * 2 + h], RES)
            rows = pl.ds(start, RES)
            factor = inverse[rows, :]
            for i in range(RES):
                value = mine[i, rows, :]
                for ref in (a, b, c):
                    value = value + ref[i, rows, :].astype(F32)
                pieces[u][i, h * RES : (h + 1) * RES, :] = (value * factor[:, i : i + 1]).astype(BF16)


def settle(place, mine, count, a, b, c):
    vmem = pl.BlockSpec(memory_space=pltpu.VMEM)
    return pl.pallas_call(
        settle_kernel,
        in_specs=[pl.BlockSpec(memory_space=pltpu.SMEM)] + [vmem] * 5,
        out_specs=[vmem] * 4,
        out_shape=[jax.ShapeDtypeStruct((RES, 2 * RES, 128), BF16)] * 4,
        scratch_shapes=[pltpu.VMEM((128, 128), F32)],
        compiler_params=pltpu.CompilerParams(vmem_limit_bytes=40 * 2**20),
        name="settle",
    )(place, mine, count, a, b, c)


def lay_kernel(place, *refs):
    out = refs[4]
    for u in range(4):
        at = pl.multiple_of(place[u * 2] * RES, RES)
        start = pl.multiple_of(place[u * 2 + 1] * 2 * RES, 2 * RES)
        out[pl.ds(at, RES), pl.ds(start, 2 * RES), :] = refs[u][...]


def lay(place, pieces):
    vmem = pl.BlockSpec(memory_space=pltpu.VMEM)
    return pl.pallas_call(
        lay_kernel,
        in_specs=[pl.BlockSpec(memory_space=pltpu.SMEM)] + [vmem] * 4,
        out_specs=vmem,
        out_shape=jax.ShapeDtypeStruct((2 * RES, 4 * RES, 128), BF16),
        compiler_params=pltpu.CompilerParams(vmem_limit_bytes=40 * 2**20),
        name="lay",
    )(place, *pieces)


def shift_pairs(n, step):
    return [(s, (s + step) % n) for s in range(n)]


def per_device(sig, mask, gain, shift, w_left, b_left, w_right, b_right, w_out):
    x = lax.axis_index("depth")
    y = lax.axis_index("row")
    col = lax.axis_index("col")
    z, core = col // 2, col % 2

    left, right = project(
        sig,
        mask,
        gain.reshape(1, 256),
        shift.reshape(1, 256),
        w_left,
        b_left.reshape(1, HID),
        w_right,
        b_right.reshape(1, HID),
    )
    mix = w_out.reshape(HID, HID, 128).transpose(2, 1, 0).reshape(128, HID * HID)

    flip = lambda v: lax.ppermute(v, "col", [(s, s ^ 1) for s in range(8)])
    rights = {0: right}
    lefts = {0: left}
    for t in (2, 1, 3):
        rights[t] = lax.ppermute(right, "row", shift_pairs(4, -t))
        lefts[t] = lax.ppermute(left, "col", shift_pairs(8, -2 * t))
    columns = []
    for t in range(4):
        columns += [rights[t], flip(rights[t])]
    rows = [lefts[t] for t in range(4)]

    def quarter(k):
        return ((x + k - z) % 4).astype(jnp.int32).reshape(1)

    got = {}
    for k in (2, 1, 3):
        (part,) = pair(False, quarter(k), rows, columns, mix)
        got[k] = lax.ppermute(part, "depth", shift_pairs(4, k))
    mine, count = pair(True, quarter(0), rows, columns, mix)

    slot = 2 * (z % 2) + core
    spots = []
    for u in range(4):
        t = ((slot + u) % 4 - y) % 4
        for h in range(2):
            spots.append(t * 32 + (h ^ core) * 16)
    pieces = settle(jnp.stack(spots).astype(jnp.int32), mine, count, got[2], got[1], got[3])

    seats, landed = [], []
    for u in range(4):
        pairs = []
        for s in range(8):
            sz, sc = s // 2, s % 2
            pairs.append((s, 2 * ((2 * (sz % 2) + sc + u) % 4) + sz // 2))
        landed.append(lax.ppermute(pieces[u], "col", pairs))
        seat = (z - u) % 4
        seats += [seat % 2, seat // 2]
    return lay(jnp.stack(seats).astype(jnp.int32), landed)


def solution(mesh):
    return jax.shard_map(
        per_device,
        mesh=mesh,
        in_specs=(
            P("depth", ("row", "col"), None),
            P("depth", ("row", "col")),
            P(),
            P(),
            P(),
            P(),
            P(),
            P(),
            P(),
        ),
        out_specs=P(("row", "depth"), "col", None),
        check_vma=False,
    )
```

```python
import functools

import jax
import jax.numpy as jnp
from jax import lax
from jax.experimental import pallas as pl
from jax.experimental.pallas import tpu as pltpu
from jax.sharding import PartitionSpec as P

F32 = jnp.float32
BF16 = jnp.bfloat16
NT = (((1,), (1,)), ((), ()))
NN = (((1,), (0,)), ((), ()))

SEQ = 256
RES = 16
HID = 32
SHARD = RES * HID
ROWS = SHARD + RES


def dot(a, b, dims):
    return lax.dot_general(a, b, dims, preferred_element_type=F32)


def project_kernel(sig, mask, gain, shift, w_left, b_left, w_right, b_right, left, right, wide, cols, turn):
    half = sig.shape[0]
    turn[...] = jnp.zeros_like(turn)
    turn[:, 0:HID] = jnp.broadcast_to(b_left[...], (128, HID))
    turn[:, HID : 2 * HID] = jnp.broadcast_to(b_right[...], (128, HID))
    bias = jnp.transpose(turn[...])[0 : 2 * HID, :]
    weights = jnp.concatenate([w_left[...], w_right[...]], axis=0)
    presence = mask[...].astype(F32)

    flat = sig[...].astype(F32).reshape(half * RES, 256)
    wide[0] = flat[:, 0:128]
    wide[1] = flat[:, 128:256]
    for r in range(RES):
        low = wide[0, pl.ds(r, half, stride=RES), :]
        high = wide[1, pl.ds(r, half, stride=RES), :]
        mean = jnp.sum(low + high, axis=1, keepdims=True) * (1.0 / 256)
        low = low - mean
        high = high - mean
        spread = jnp.sum(low * low + high * high, axis=1, keepdims=True) * (1.0 / 256)
        scale = lax.rsqrt(spread + 1e-5)
        low = low * scale * gain[:, 0:128] + shift[:, 0:128]
        high = high * scale * gain[:, 128:256] + shift[:, 128:256]
        normed = jnp.concatenate([low.astype(BF16), high.astype(BF16)], axis=1)
        both = (dot(weights, normed, NT) + bias) * presence[r : r + 1, :]
        left[r * HID : (r + 1) * HID, :] = both[0:HID].astype(BF16)
        cols[r * HID : (r + 1) * HID, :] = both[HID : 2 * HID]
    for d in range(HID):
        right[d * RES : (d + 1) * RES, :] = cols[pl.ds(d, RES, stride=HID), :].astype(BF16)
    left[SHARD:ROWS, :] = mask[...]
    right[SHARD:ROWS, :] = mask[...]


def project(sig, mask, gain, shift, w_left, b_left, w_right, b_right):
    steps = 2
    half = SEQ // steps
    whole = lambda shape: pl.BlockSpec(shape, lambda s: (0,) * len(shape))
    return pl.pallas_call(
        project_kernel,
        grid=(steps,),
        in_specs=[
            pl.BlockSpec((half, RES, 256), lambda s: (s, 0, 0)),
            pl.BlockSpec((RES, half), lambda s: (0, s)),
            whole((1, 256)),
            whole((1, 256)),
            whole((HID, 256)),
            whole((1, HID)),
            whole((HID, 256)),
            whole((1, HID)),
        ],
        out_specs=[pl.BlockSpec((ROWS, half), lambda s: (0, s))] * 2,
        out_shape=[jax.ShapeDtypeStruct((ROWS, SEQ), BF16)] * 2,
        scratch_shapes=[
            pltpu.VMEM((2, half * RES, 128), F32),
            pltpu.VMEM((SHARD, half), F32),
            pltpu.VMEM((128, 128), F32),
        ],
        compiler_params=pltpu.CompilerParams(vmem_limit_bytes=56 * 2**20),
        name="project",
    )(sig, mask, gain, shift, w_left, b_left, w_right, b_right)


def order_kernel(w_out, mix, rows, sorted_rows):
    rows[...] = w_out[...].astype(F32)
    for d in range(HID):
        sorted_rows[d * HID : (d + 1) * HID, :] = rows[pl.ds(d, HID, stride=HID), :]
    for b in range(8):
        mix[:, b * 128 : (b + 1) * 128] = jnp.transpose(sorted_rows[b * 128 : (b + 1) * 128, :]).astype(BF16)


def order(w_out):
    vmem = pl.BlockSpec(memory_space=pltpu.VMEM)
    return pl.pallas_call(
        order_kernel,
        in_specs=[vmem],
        out_specs=vmem,
        out_shape=jax.ShapeDtypeStruct((128, HID * HID), BF16),
        scratch_shapes=[pltpu.VMEM((HID * HID, 128), F32)] * 2,
        compiler_params=pltpu.CompilerParams(vmem_limit_bytes=8 * 2**20),
        name="order",
    )(w_out)


def pair_kernel(own, place, *refs):
    lefts, rights, mix = refs[0:4], refs[4:12], refs[12]
    if own:
        out, count, outer, chosen = refs[13:]
    else:
        out, outer, chosen = refs[13:]
    which = place[0]
    for t in range(4):

        @pl.when(which == t)
        def _():
            chosen[...] = lefts[t][...]

    @pl.loop(0, HID // 2, unroll=True)
    def _(step):
        parts = []
        for dd in range(2):
            start = pl.multiple_of(step * 2 * RES + dd * RES, RES)
            for ref in rights:
                parts.append(ref[pl.ds(start, RES), :])
        block = jnp.concatenate(parts, axis=0)
        prod = dot(chosen[0:SHARD, :], block, NT).astype(BF16)
        for dd in range(2):
            at = pl.multiple_of(step * 2 * HID + dd * HID, HID)
            for i in range(RES):
                outer[i // 2, pl.ds(at, HID), (i % 2) * 128 : (i % 2) * 128 + 128] = prod[
                    i * HID : (i + 1) * HID, dd * 128 : (dd + 1) * 128
                ]

    @pl.loop(0, RES // 2, unroll=True)
    def _(pair):
        mixed = dot(mix[...], outer[pair], NN)
        for ii in range(2):
            out[pair * 2 + ii] = jnp.transpose(mixed[:, ii * 128 : (ii + 1) * 128]).astype(out.dtype)

    weights = jnp.concatenate([ref[SHARD:ROWS, :] for ref in rights], axis=0)
    tally = jnp.concatenate([chosen[SHARD:ROWS, :], jnp.zeros((128 - RES, SEQ), BF16)], axis=0)
    tally = dot(weights, tally, NT)
    if own:
        count[...] = tally
    else:
        high = tally.astype(BF16)
        out[RES] = high
        out[RES + 1] = (tally - high.astype(F32)).astype(BF16)


def pair(own, place, lefts, rights, mix):
    vmem = pl.BlockSpec(memory_space=pltpu.VMEM)
    if own:
        out_shape = [
            jax.ShapeDtypeStruct((RES, 128, 128), F32),
            jax.ShapeDtypeStruct((128, 128), F32),
        ]
    else:
        out_shape = [jax.ShapeDtypeStruct((RES + 2, 128, 128), BF16)]
    return pl.pallas_call(
        functools.partial(pair_kernel, own),
        in_specs=[pl.BlockSpec(memory_space=pltpu.SMEM)] + [vmem] * 13,
        out_specs=[vmem] * len(out_shape),
        out_shape=out_shape,
        scratch_shapes=[
            pltpu.VMEM((RES // 2, HID * HID, 256), BF16),
            pltpu.VMEM((ROWS, SEQ), BF16),
        ],
        compiler_params=pltpu.CompilerParams(vmem_limit_bytes=16 * 2**20),
        cost_estimate=pl.CostEstimate(
            flops=2 * SHARD * SHARD * 8 * SEQ + 2 * 128 * 16 * 128 * 1024,
            bytes_accessed=5 * 2**20,
            transcendentals=0,
        ),
        name="pair",
    )(place, *lefts, *rights, mix)


def settle_kernel(place, mine, count, a, b, c, pieces, inverse):
    total = count[...]
    for ref in (a, b, c):
        total = total + (ref[RES].astype(F32) + ref[RES + 1].astype(F32))
    inverse[...] = 1.0 / jnp.maximum(total, 1.0)
    for p in range(4):
        for h in range(2):
            rows = pl.ds(pl.multiple_of(place[p * 2 + h], RES), RES)
            factor = inverse[rows, :]
            for i in range(RES):
                value = mine[i, rows, :]
                for ref in (a, b, c):
                    value = value + ref[i, rows, :].astype(F32)
                pieces[p, i, h * RES : (h + 1) * RES, :] = (value * factor[:, i : i + 1]).astype(BF16)


def settle(place, mine, count, a, b, c):
    vmem = pl.BlockSpec(memory_space=pltpu.VMEM)
    return pl.pallas_call(
        settle_kernel,
        in_specs=[pl.BlockSpec(memory_space=pltpu.SMEM)] + [vmem] * 5,
        out_specs=vmem,
        out_shape=jax.ShapeDtypeStruct((4, RES, 2 * RES, 128), BF16),
        scratch_shapes=[pltpu.VMEM((128, 128), F32)],
        compiler_params=pltpu.CompilerParams(vmem_limit_bytes=8 * 2**20),
        name="settle",
    )(place, mine, count, a, b, c)


def lay_kernel(place, kept, given, out):
    mine = pl.ds(pl.multiple_of(place[0], RES), RES)
    theirs = pl.ds(pl.multiple_of(RES - place[0], RES), RES)
    for half in range(2):
        span = slice(half * 2 * RES, (half + 1) * 2 * RES)
        out[mine, span, :] = kept[half]
        out[theirs, span, :] = given[half]


def lay(place, kept, given):
    vmem = pl.BlockSpec(memory_space=pltpu.VMEM)
    return pl.pallas_call(
        lay_kernel,
        in_specs=[pl.BlockSpec(memory_space=pltpu.SMEM)] + [vmem] * 2,
        out_specs=vmem,
        out_shape=jax.ShapeDtypeStruct((2 * RES, 4 * RES, 128), BF16),
        compiler_params=pltpu.CompilerParams(vmem_limit_bytes=8 * 2**20),
        name="lay",
    )(place, kept, given)


def shift_pairs(n, step):
    return [(s, (s + step) % n) for s in range(n)]


def per_device(sig, mask, gain, shift, w_left, b_left, w_right, b_right, w_out):
    x = lax.axis_index("depth")
    y = lax.axis_index("row")
    col = lax.axis_index("col")
    z, core = col >> 1, col & 1

    left, right = project(
        sig,
        mask.T,
        gain.reshape(1, 256),
        shift.reshape(1, 256),
        w_left.T,
        b_left.reshape(1, HID),
        w_right.T,
        b_right.reshape(1, HID),
    )

    flip = lambda v: lax.ppermute(v, "col", [(s, s ^ 1) for s in range(8)])
    rights = {0: right}
    lefts = {0: left}
    for t in (2, 1, 3):
        rights[t] = lax.ppermute(right, "row", shift_pairs(4, -t))
        lefts[t] = lax.ppermute(left, "col", shift_pairs(8, -2 * t))
    mix, rights[2] = lax.optimization_barrier((order(w_out), rights[2]))
    columns = []
    for t in range(4):
        columns += [rights[t], flip(rights[t])]
    rows = [lefts[t] for t in range(4)]

    def quarter(k):
        return ((x + k - z) & 3).astype(jnp.int32).reshape(1)

    got = {}
    for k in (2, 1, 3):
        (part,) = pair(False, quarter(k), rows, columns, mix)
        got[k] = lax.ppermute(part, "depth", shift_pairs(4, k))
    mine, count = pair(True, quarter(0), rows, columns, mix)

    spots = []
    for p in range(4):
        t = (p + 2 * core - y) & 3
        for h in range(2):
            spots.append(t * 32 + (h ^ core) * 16)
    pieces = settle(jnp.stack(spots).astype(jnp.int32), mine, count, got[2], got[1], got[3])
    landed = lax.all_to_all(
        pieces, "col", 0, 0, axis_index_groups=[[0, 2, 4, 6], [5, 7, 1, 3]], tiled=True
    )
    given = flip(landed[2:4])
    return lay((core * RES).astype(jnp.int32).reshape(1), landed[0:2], given)


def solution(mesh):
    return jax.shard_map(
        per_device,
        mesh=mesh,
        in_specs=(
            P("depth", ("row", "col"), None),
            P("depth", ("row", "col")),
            P(),
            P(),
            P(),
            P(),
            P(),
            P(),
            P(),
        ),
        out_specs=P(("row", "depth"), "col", None),
        check_vma=False,
    )
```

```python
import functools

import jax
import jax.numpy as jnp
from jax import lax
from jax.experimental import pallas as pl
from jax.experimental.pallas import tpu as pltpu
from jax.sharding import PartitionSpec as P

F32 = jnp.float32
BF16 = jnp.bfloat16
NT = (((1,), (1,)), ((), ()))
NN = (((1,), (0,)), ((), ()))

SEQ = 256
RES = 16
HID = 32
SHARD = RES * HID
ROWS = SHARD + RES
WIDE = 8 * RES
BIG = 56 * 2**20


def dot(a, b, dims):
    return lax.dot_general(a, b, dims, preferred_element_type=F32)


def project_kernel(sig, mask, gain, shift, w_left, b_left, w_right, b_right, left, right, wide, cols, turn):
    half = sig.shape[0]
    turn[...] = jnp.zeros_like(turn)
    turn[:, 0:HID] = jnp.broadcast_to(b_left[...], (128, HID))
    turn[:, HID : 2 * HID] = jnp.broadcast_to(b_right[...], (128, HID))
    bias = jnp.transpose(turn[...])[0 : 2 * HID, :]
    weights = jnp.concatenate([w_left[...], w_right[...]], axis=0)
    presence = mask[...].astype(F32)

    flat = sig[...].astype(F32).reshape(half * RES, 256)
    wide[0] = flat[:, 0:128]
    wide[1] = flat[:, 128:256]
    for r in range(RES):
        low = wide[0, pl.ds(r, half, stride=RES), :]
        high = wide[1, pl.ds(r, half, stride=RES), :]
        mean = jnp.sum(low + high, axis=1, keepdims=True) * (1.0 / 256)
        low = low - mean
        high = high - mean
        spread = jnp.sum(low * low + high * high, axis=1, keepdims=True) * (1.0 / 256)
        scale = lax.rsqrt(spread + 1e-5)
        low = low * scale * gain[:, 0:128] + shift[:, 0:128]
        high = high * scale * gain[:, 128:256] + shift[:, 128:256]
        normed = jnp.concatenate([low.astype(BF16), high.astype(BF16)], axis=1)
        both = (dot(weights, normed, NT) + bias) * presence[r : r + 1, :]
        left[r * HID : (r + 1) * HID, :] = both[0:HID].astype(BF16)
        cols[r * HID : (r + 1) * HID, :] = both[HID : 2 * HID]
    for d in range(HID):
        right[d * RES : (d + 1) * RES, :] = cols[pl.ds(d, RES, stride=HID), :].astype(BF16)
    left[SHARD:ROWS, :] = mask[...]
    right[SHARD:ROWS, :] = mask[...]


def project(sig, mask, gain, shift, w_left, b_left, w_right, b_right):
    steps = 2
    half = SEQ // steps
    whole = lambda shape: pl.BlockSpec(shape, lambda s: (0,) * len(shape))
    return pl.pallas_call(
        project_kernel,
        grid=(steps,),
        in_specs=[
            pl.BlockSpec((half, RES, 256), lambda s: (s, 0, 0)),
            pl.BlockSpec((RES, half), lambda s: (0, s)),
            whole((1, 256)),
            whole((1, 256)),
            whole((HID, 256)),
            whole((1, HID)),
            whole((HID, 256)),
            whole((1, HID)),
        ],
        out_specs=[pl.BlockSpec((ROWS, half), lambda s: (0, s))] * 2,
        out_shape=[jax.ShapeDtypeStruct((ROWS, SEQ), BF16)] * 2,
        scratch_shapes=[
            pltpu.VMEM((2, half * RES, 128), F32),
            pltpu.VMEM((SHARD, half), F32),
            pltpu.VMEM((128, 128), F32),
        ],
        compiler_params=pltpu.CompilerParams(vmem_limit_bytes=BIG),
        name="project",
    )(sig, mask, gain, shift, w_left, b_left, w_right, b_right)


def order_kernel(w_out, left_in, right_in, mix, left, right, rows, sorted_rows):
    rows[...] = w_out[...].astype(F32)
    for d in range(HID):
        sorted_rows[d * HID : (d + 1) * HID, :] = rows[pl.ds(d, HID, stride=HID), :]
    for b in range(8):
        mix[:, b * 128 : (b + 1) * 128] = jnp.transpose(sorted_rows[b * 128 : (b + 1) * 128, :]).astype(BF16)
    left[...] = left_in[...]
    right[...] = right_in[...]


def order(w_out, left, right):
    vmem = pl.BlockSpec(memory_space=pltpu.VMEM)
    return pl.pallas_call(
        order_kernel,
        in_specs=[vmem] * 3,
        out_specs=[vmem] * 3,
        out_shape=[jax.ShapeDtypeStruct((128, HID * HID), BF16)] + [jax.ShapeDtypeStruct((ROWS, SEQ), BF16)] * 2,
        scratch_shapes=[pltpu.VMEM((HID * HID, 128), F32)] * 2,
        compiler_params=pltpu.CompilerParams(vmem_limit_bytes=8 * 2**20),
        name="order",
    )(w_out, left, right)


def pair_kernel(first, place, *refs):
    if first:
        lefts, rights, mix, out, packed, outer = refs[0:4], refs[4:12], *refs[12:]
        for t in range(4):
            packed[t] = lefts[t][...]
        for v in range(8):
            packed[4 + v] = rights[v][...]
        outs = [out]
    else:
        packed, mix, *outs, own, count, outer = refs

    def right(v, rows):
        return rights[v][rows, :] if first else packed[4 + v, rows, :]

    weights = jnp.concatenate([right(v, slice(SHARD, ROWS)) for v in range(8)], axis=0)
    for q in range(1 if first else 3):
        which = place[q]
        rows = packed[which, 0:SHARD, :]
        for step in range(HID // 2):
            parts = []
            for dd in range(2):
                start = (step * 2 + dd) * RES
                parts += [right(v, slice(start, start + RES)) for v in range(8)]
            prod = dot(rows, jnp.concatenate(parts, axis=0), NT).astype(BF16)
            for dd in range(2):
                at = (step * 2 + dd) * HID
                for i in range(RES):
                    outer[i // 2, at : at + HID, (i % 2) * 128 : (i % 2) * 128 + 128] = prod[
                        i * HID : (i + 1) * HID, dd * 128 : (dd + 1) * 128
                    ]
        for pair in range(RES // 2):
            mixed = dot(mix[...], outer[pair], NN)
            for ii in range(2):
                at = (pair * 2 + ii) * WIDE
                turned = jnp.transpose(mixed[:, ii * 128 : (ii + 1) * 128])
                if q < len(outs):
                    outs[q][at : at + WIDE, :] = turned.astype(BF16)
                else:
                    own[at : at + WIDE, :] = turned
        tally = dot(packed[which, SHARD:ROWS, :], weights, NT)
        if q < len(outs):
            high = tally.astype(BF16)
            outs[q][RES * WIDE : RES * WIDE + RES, :] = high
            outs[q][RES * WIDE + RES : RES * WIDE + 2 * RES, :] = (tally - high.astype(F32)).astype(BF16)
        else:
            count[...] = tally


def pair(first, place, *args):
    vmem = pl.BlockSpec(memory_space=pltpu.VMEM)
    part = jax.ShapeDtypeStruct((RES * WIDE + 2 * RES, 128), BF16)
    if first:
        out_shape = [part, jax.ShapeDtypeStruct((12, ROWS, SEQ), BF16)]
    else:
        out_shape = [
            part,
            part,
            jax.ShapeDtypeStruct((RES * WIDE, 128), F32),
            jax.ShapeDtypeStruct((RES, 128), F32),
        ]
    return pl.pallas_call(
        functools.partial(pair_kernel, first),
        in_specs=[pl.BlockSpec(memory_space=pltpu.SMEM)] + [vmem] * len(args),
        out_specs=[vmem] * len(out_shape),
        out_shape=out_shape,
        scratch_shapes=[pltpu.VMEM((RES // 2, HID * HID, 256), BF16)],
        compiler_params=pltpu.CompilerParams(vmem_limit_bytes=12 * 2**20),
        cost_estimate=pl.CostEstimate(flops=2**28, bytes_accessed=2**16, transcendentals=0),
        name="pair_first" if first else "pair_rest",
    )(place, *args)


def fold_kernel(mine, count, part, total, total_count):
    end = RES * WIDE
    total[...] = mine[...] + part[0:end, :].astype(F32)
    high, low = part[end : end + RES, :].astype(F32), part[end + RES : end + 2 * RES, :].astype(F32)
    total_count[...] = count[...] + (high + low)


def fold(mine, count, part):
    vmem = pl.BlockSpec(memory_space=pltpu.VMEM)
    return pl.pallas_call(
        fold_kernel,
        in_specs=[vmem] * 3,
        out_specs=[vmem] * 2,
        out_shape=[jax.ShapeDtypeStruct(mine.shape, F32), jax.ShapeDtypeStruct(count.shape, F32)],
        compiler_params=pltpu.CompilerParams(vmem_limit_bytes=8 * 2**20),
        name="fold",
    )(mine, count, part)


def settle_kernel(place, mine, count, a, b, pieces, inverse):
    end = RES * WIDE
    total = count[...]
    for ref in (a, b):
        total = total + (ref[end : end + RES, :].astype(F32) + ref[end + RES : end + 2 * RES, :].astype(F32))
    inverse[0:RES, :] = 1.0 / jnp.maximum(total, 1.0)
    inverse[...] = jnp.transpose(inverse[...])
    for p in range(4):
        for h in range(2):
            start = pl.multiple_of(place[p * 2 + h], RES)
            factor = inverse[pl.ds(start, RES), :]
            for i in range(RES):
                rows = pl.ds(pl.multiple_of(start + i * WIDE, RES), RES)
                value = mine[rows, :] + (a[rows, :].astype(F32) + b[rows, :].astype(F32))
                pieces[p, i, h * RES : (h + 1) * RES, :] = (value * factor[:, i : i + 1]).astype(BF16)


def settle(place, mine, count, a, b):
    vmem = pl.BlockSpec(memory_space=pltpu.VMEM)
    return pl.pallas_call(
        settle_kernel,
        in_specs=[pl.BlockSpec(memory_space=pltpu.SMEM)] + [vmem] * 4,
        out_specs=vmem,
        out_shape=jax.ShapeDtypeStruct((4, RES, 2 * RES, 128), BF16),
        scratch_shapes=[pltpu.VMEM((128, 128), F32)],
        compiler_params=pltpu.CompilerParams(vmem_limit_bytes=8 * 2**20),
        name="settle",
    )(place, mine, count, a, b)


def lay_kernel(place, kept, given, out):
    mine = pl.ds(pl.multiple_of(place[0], RES), RES)
    theirs = pl.ds(pl.multiple_of(RES - place[0], RES), RES)
    for half in range(2):
        span = slice(half * 2 * RES, (half + 1) * 2 * RES)
        out[mine, span, :] = kept[half]
        out[theirs, span, :] = given[half]


def lay(place, kept, given):
    vmem = pl.BlockSpec(memory_space=pltpu.VMEM)
    return pl.pallas_call(
        lay_kernel,
        in_specs=[pl.BlockSpec(memory_space=pltpu.SMEM)] + [vmem] * 2,
        out_specs=vmem,
        out_shape=jax.ShapeDtypeStruct((2 * RES, 4 * RES, 128), BF16),
        compiler_params=pltpu.CompilerParams(vmem_limit_bytes=8 * 2**20),
        name="lay",
    )(place, kept, given)


def shift_pairs(n, step):
    return [(s, (s + step) % n) for s in range(n)]


def per_device(sig, mask, gain, shift, w_left, b_left, w_right, b_right, w_out):
    x = lax.axis_index("depth")
    y = lax.axis_index("row")
    col = lax.axis_index("col")
    z, core = col >> 1, col & 1

    left, right = project(
        sig,
        mask.T,
        gain.reshape(1, 256),
        shift.reshape(1, 256),
        w_left.T,
        b_left.reshape(1, HID),
        w_right.T,
        b_right.reshape(1, HID),
    )

    flip = lambda v: lax.ppermute(v, "col", [(s, s ^ 1) for s in range(8)])
    rights = {0: right}
    lefts = {0: left}
    for t in (2, 1, 3):
        rights[t] = lax.ppermute(right, "row", shift_pairs(4, -t))
        lefts[t] = lax.ppermute(left, "col", shift_pairs(8, -2 * t))
    mix, lefts[0], rights[0], rights[2] = lax.optimization_barrier((*order(w_out, left, right), rights[2]))
    columns = []
    for t in range(4):
        columns += [rights[t], flip(rights[t])]
    rows = [lefts[t] for t in range(4)]

    quarter = lambda *ks: jnp.stack([(x + k - z) & 3 for k in ks]).astype(jnp.int32)
    got = {}
    part, packed = pair(True, quarter(2), *rows, *columns, mix)
    got[2] = lax.ppermute(part, "depth", shift_pairs(4, 2))
    ahead, behind, mine, count = pair(False, quarter(1, 3, 0), packed, mix)
    got[1] = lax.ppermute(ahead, "depth", shift_pairs(4, 1))
    got[3] = lax.ppermute(behind, "depth", shift_pairs(4, 3))

    spots = []
    for p in range(4):
        t = (p + 2 * core - y) & 3
        for h in range(2):
            spots.append(t * 32 + (h ^ core) * 16)
    mine, count = fold(mine, count, got[2])
    pieces = settle(jnp.stack(spots).astype(jnp.int32), mine, count, got[1], got[3])
    landed = lax.all_to_all(
        pieces, "col", 0, 0, axis_index_groups=[[0, 2, 4, 6], [5, 7, 1, 3]], tiled=True
    )
    given = flip(landed[2:4])
    return lay((core * RES).astype(jnp.int32).reshape(1), landed[0:2], given)


def solution(mesh):
    return jax.shard_map(
        per_device,
        mesh=mesh,
        in_specs=(
            P("depth", ("row", "col"), None),
            P("depth", ("row", "col")),
            P(),
            P(),
            P(),
            P(),
            P(),
            P(),
            P(),
        ),
        out_specs=P(("row", "depth"), "col", None),
        check_vma=False,
    )
```

```python
import functools

import jax
import jax.numpy as jnp
from jax import lax
from jax.experimental import pallas as pl
from jax.experimental.pallas import tpu as pltpu
from jax.sharding import PartitionSpec as P

F32 = jnp.float32
BF16 = jnp.bfloat16
NT = (((1,), (1,)), ((), ()))
NN = (((1,), (0,)), ((), ()))

SEQ = 256
RES = 16
HID = 32
SHARD = RES * HID
ROWS = SHARD + RES
WIDE = 8 * RES
BIG = 56 * 2**20


def dot(a, b, dims):
    return lax.dot_general(a, b, dims, preferred_element_type=F32)


def project_kernel(sig, mask, gain, shift, w_left, b_left, w_right, b_right, left, right, wide, cols, turn):
    half = sig.shape[0]
    turn[...] = jnp.zeros_like(turn)
    turn[:, 0:HID] = jnp.broadcast_to(b_left[...], (128, HID))
    turn[:, HID : 2 * HID] = jnp.broadcast_to(b_right[...], (128, HID))
    bias = jnp.transpose(turn[...])[0 : 2 * HID, :]
    weights = jnp.concatenate([w_left[...], w_right[...]], axis=0)
    presence = mask[...].astype(F32)

    flat = sig[...].astype(F32).reshape(half * RES, 256)
    wide[0] = flat[:, 0:128]
    wide[1] = flat[:, 128:256]
    for r in range(RES):
        low = wide[0, pl.ds(r, half, stride=RES), :]
        high = wide[1, pl.ds(r, half, stride=RES), :]
        mean = jnp.sum(low + high, axis=1, keepdims=True) * (1.0 / 256)
        low = low - mean
        high = high - mean
        spread = jnp.sum(low * low + high * high, axis=1, keepdims=True) * (1.0 / 256)
        scale = lax.rsqrt(spread + 1e-5)
        low = low * scale * gain[:, 0:128] + shift[:, 0:128]
        high = high * scale * gain[:, 128:256] + shift[:, 128:256]
        normed = jnp.concatenate([low.astype(BF16), high.astype(BF16)], axis=1)
        both = (dot(weights, normed, NT) + bias) * presence[r : r + 1, :]
        left[r * HID : (r + 1) * HID, :] = both[0:HID].astype(BF16)
        cols[r * HID : (r + 1) * HID, :] = both[HID : 2 * HID]
    for d in range(HID):
        right[d * RES : (d + 1) * RES, :] = cols[pl.ds(d, RES, stride=HID), :].astype(BF16)
    left[SHARD:ROWS, :] = mask[...]
    right[SHARD:ROWS, :] = mask[...]


def project(sig, mask, gain, shift, w_left, b_left, w_right, b_right):
    steps = 2
    half = SEQ // steps
    whole = lambda shape: pl.BlockSpec(shape, lambda s: (0,) * len(shape))
    return pl.pallas_call(
        project_kernel,
        grid=(steps,),
        in_specs=[
            pl.BlockSpec((half, RES, 256), lambda s: (s, 0, 0)),
            pl.BlockSpec((RES, half), lambda s: (0, s)),
            whole((1, 256)),
            whole((1, 256)),
            whole((HID, 256)),
            whole((1, HID)),
            whole((HID, 256)),
            whole((1, HID)),
        ],
        out_specs=[pl.BlockSpec((ROWS, half), lambda s: (0, s))] * 2,
        out_shape=[jax.ShapeDtypeStruct((ROWS, SEQ), BF16)] * 2,
        scratch_shapes=[
            pltpu.VMEM((2, half * RES, 128), F32),
            pltpu.VMEM((SHARD, half), F32),
            pltpu.VMEM((128, 128), F32),
        ],
        compiler_params=pltpu.CompilerParams(vmem_limit_bytes=BIG),
        name="project",
    )(sig, mask, gain, shift, w_left, b_left, w_right, b_right)


def order_kernel(w_out, left_in, right_in, mix, left, right, rows, sorted_rows):
    rows[...] = w_out[...].astype(F32)
    for d in range(HID):
        sorted_rows[d * HID : (d + 1) * HID, :] = rows[pl.ds(d, HID, stride=HID), :]
    for b in range(8):
        mix[:, b * 128 : (b + 1) * 128] = jnp.transpose(sorted_rows[b * 128 : (b + 1) * 128, :]).astype(BF16)
    left[...] = left_in[...]
    right[...] = right_in[...]


def order(w_out, left, right):
    vmem = pl.BlockSpec(memory_space=pltpu.VMEM)
    return pl.pallas_call(
        order_kernel,
        in_specs=[vmem] * 3,
        out_specs=[vmem] * 3,
        out_shape=[jax.ShapeDtypeStruct((128, HID * HID), BF16)] + [jax.ShapeDtypeStruct((ROWS, SEQ), BF16)] * 2,
        scratch_shapes=[pltpu.VMEM((HID * HID, 128), F32)] * 2,
        compiler_params=pltpu.CompilerParams(vmem_limit_bytes=8 * 2**20),
        name="order",
    )(w_out, left, right)


def choose_kernel(which, a, b, out):
    @pl.when(which[0] == 0)
    def _():
        out[...] = a[...]

    @pl.when(which[0] != 0)
    def _():
        out[...] = b[...]


def choose(which, a, b):
    vmem = pl.BlockSpec(memory_space=pltpu.VMEM)
    return pl.pallas_call(
        choose_kernel,
        in_specs=[pl.BlockSpec(memory_space=pltpu.SMEM)] + [vmem] * 2,
        out_specs=vmem,
        out_shape=jax.ShapeDtypeStruct(a.shape, a.dtype),
        compiler_params=pltpu.CompilerParams(vmem_limit_bytes=4 * 2**20),
        name="choose",
    )(which, a, b)


def pair_kernel(first, place, *refs):
    if first:
        lefts, rights, mix, out, packed, outer = refs[0:4], refs[4:12], *refs[12:]
        for t in range(4):
            packed[t] = lefts[t][...]
        for v in range(8):
            packed[4 + v] = rights[v][...]
        outs = [out]
    else:
        packed, mix, *outs, own, count, outer = refs

    def right(v, rows):
        return rights[v][rows, :] if first else packed[4 + v, rows, :]

    weights = jnp.concatenate([right(v, slice(SHARD, ROWS)) for v in range(8)], axis=0)
    for q in range(1 if first else 3):
        which = place[q]
        rows = packed[which, 0:SHARD, :]
        for step in range(HID // 2):
            parts = []
            for dd in range(2):
                start = (step * 2 + dd) * RES
                parts += [right(v, slice(start, start + RES)) for v in range(8)]
            prod = dot(rows, jnp.concatenate(parts, axis=0), NT).astype(BF16)
            for dd in range(2):
                at = (step * 2 + dd) * HID
                for i in range(RES):
                    outer[i // 2, at : at + HID, (i % 2) * 128 : (i % 2) * 128 + 128] = prod[
                        i * HID : (i + 1) * HID, dd * 128 : (dd + 1) * 128
                    ]
        for pair in range(RES // 2):
            mixed = dot(mix[...], outer[pair], NN)
            for ii in range(2):
                at = (pair * 2 + ii) * WIDE
                turned = jnp.transpose(mixed[:, ii * 128 : (ii + 1) * 128])
                if q < len(outs):
                    outs[q][at : at + WIDE, :] = turned.astype(BF16)
                else:
                    own[at : at + WIDE, :] = turned
        tally = dot(packed[which, SHARD:ROWS, :], weights, NT)
        if q < len(outs):
            high = tally.astype(BF16)
            outs[q][RES * WIDE : RES * WIDE + RES, :] = high
            outs[q][RES * WIDE + RES : RES * WIDE + 2 * RES, :] = (tally - high.astype(F32)).astype(BF16)
        else:
            count[...] = tally


def pair(first, place, *args):
    vmem = pl.BlockSpec(memory_space=pltpu.VMEM)
    part = jax.ShapeDtypeStruct((RES * WIDE + 2 * RES, 128), BF16)
    if first:
        out_shape = [part, jax.ShapeDtypeStruct((12, ROWS, SEQ), BF16)]
    else:
        out_shape = [
            part,
            part,
            jax.ShapeDtypeStruct((RES * WIDE, 128), F32),
            jax.ShapeDtypeStruct((RES, 128), F32),
        ]
    return pl.pallas_call(
        functools.partial(pair_kernel, first),
        in_specs=[pl.BlockSpec(memory_space=pltpu.SMEM)] + [vmem] * len(args),
        out_specs=[vmem] * len(out_shape),
        out_shape=out_shape,
        scratch_shapes=[pltpu.VMEM((RES // 2, HID * HID, 256), BF16)],
        compiler_params=pltpu.CompilerParams(vmem_limit_bytes=12 * 2**20),
        cost_estimate=pl.CostEstimate(flops=2**28, bytes_accessed=2**16, transcendentals=0),
        name="pair_first" if first else "pair_rest",
    )(place, *args)


def fold_kernel(mine, count, part, total, total_count):
    end = RES * WIDE
    total[...] = mine[...] + part[0:end, :].astype(F32)
    high, low = part[end : end + RES, :].astype(F32), part[end + RES : end + 2 * RES, :].astype(F32)
    total_count[...] = count[...] + (high + low)


def fold(mine, count, part):
    vmem = pl.BlockSpec(memory_space=pltpu.VMEM)
    return pl.pallas_call(
        fold_kernel,
        in_specs=[vmem] * 3,
        out_specs=[vmem] * 2,
        out_shape=[jax.ShapeDtypeStruct(mine.shape, F32), jax.ShapeDtypeStruct(count.shape, F32)],
        compiler_params=pltpu.CompilerParams(vmem_limit_bytes=8 * 2**20),
        name="fold",
    )(mine, count, part)


def settle_kernel(place, mine, count, a, b, pieces, inverse):
    end = RES * WIDE
    total = count[...]
    for ref in (a, b):
        total = total + (ref[end : end + RES, :].astype(F32) + ref[end + RES : end + 2 * RES, :].astype(F32))
    inverse[0:RES, :] = 1.0 / jnp.maximum(total, 1.0)
    inverse[...] = jnp.transpose(inverse[...])
    for p in range(4):
        for h in range(2):
            start = pl.multiple_of(place[p * 2 + h], RES)
            factor = inverse[pl.ds(start, RES), :]
            for i in range(RES):
                rows = pl.ds(pl.multiple_of(start + i * WIDE, RES), RES)
                value = mine[rows, :] + (a[rows, :].astype(F32) + b[rows, :].astype(F32))
                pieces[p, i, h * RES : (h + 1) * RES, :] = (value * factor[:, i : i + 1]).astype(BF16)


def settle(place, mine, count, a, b):
    vmem = pl.BlockSpec(memory_space=pltpu.VMEM)
    return pl.pallas_call(
        settle_kernel,
        in_specs=[pl.BlockSpec(memory_space=pltpu.SMEM)] + [vmem] * 4,
        out_specs=vmem,
        out_shape=jax.ShapeDtypeStruct((4, RES, 2 * RES, 128), BF16),
        scratch_shapes=[pltpu.VMEM((128, 128), F32)],
        compiler_params=pltpu.CompilerParams(vmem_limit_bytes=8 * 2**20),
        name="settle",
    )(place, mine, count, a, b)


def lay_kernel(place, kept, given, out):
    mine = pl.ds(pl.multiple_of(place[0], RES), RES)
    theirs = pl.ds(pl.multiple_of(RES - place[0], RES), RES)
    for half in range(2):
        span = slice(half * 2 * RES, (half + 1) * 2 * RES)
        out[mine, span, :] = kept[half]
        out[theirs, span, :] = given[half]


def lay(place, kept, given):
    vmem = pl.BlockSpec(memory_space=pltpu.VMEM)
    return pl.pallas_call(
        lay_kernel,
        in_specs=[pl.BlockSpec(memory_space=pltpu.SMEM)] + [vmem] * 2,
        out_specs=vmem,
        out_shape=jax.ShapeDtypeStruct((2 * RES, 4 * RES, 128), BF16),
        compiler_params=pltpu.CompilerParams(vmem_limit_bytes=8 * 2**20),
        name="lay",
    )(place, kept, given)


def shift_pairs(n, step):
    return [(s, (s + step) % n) for s in range(n)]


def per_device(sig, mask, gain, shift, w_left, b_left, w_right, b_right, w_out):
    x = lax.axis_index("depth")
    y = lax.axis_index("row")
    col = lax.axis_index("col")
    z, core = col >> 1, col & 1

    left, right = project(
        sig,
        mask.T,
        gain.reshape(1, 256),
        shift.reshape(1, 256),
        w_left.T,
        b_left.reshape(1, HID),
        w_right.T,
        b_right.reshape(1, HID),
    )

    flip = lambda v: lax.ppermute(v, "col", [(s, s ^ 1) for s in range(8)])
    rights = {0: right}
    lefts = {0: left}
    for t in (1, 3):
        rights[t] = lax.ppermute(right, "row", shift_pairs(4, -t))
        lefts[t] = lax.ppermute(left, "col", shift_pairs(8, -2 * t))
    def relay(near, axis):
        pairs = []
        for sy in range(4):
            for sz in range(4):
                for sc in range(2):
                    step = 2 * sc - 1
                    dy, dz = ((sy + step) % 4, sz) if axis == "row" else (sy, (sz + step) % 4)
                    pairs.append((8 * sy + 2 * sz + sc, 8 * dy + 2 * dz + sc))
        return lax.ppermute(near, ("row", "col"), pairs)

    which = core.astype(jnp.int32).reshape(1)
    rights[2] = relay(choose(which, rights[1], rights[3]), "row")
    passed = choose(which, lefts[1], lefts[3])
    own, rights[1], rights[3], passed = lax.optimization_barrier((right, rights[1], rights[3], passed))
    lefts[2] = relay(passed, "col")
    late_left, late_right, rights[2] = lax.optimization_barrier((left, right, rights[2]))
    mix, lefts[0], rights[0] = order(w_out, late_left, late_right)
    columns = []
    for t in range(4):
        columns += [rights[t], flip(rights[t] if t else own)]
    rows = [lefts[t] for t in range(4)]

    quarter = lambda *ks: jnp.stack([(x + k - z) & 3 for k in ks]).astype(jnp.int32)
    got = {}
    part, packed = pair(True, quarter(2), *rows, *columns, mix)
    got[2] = lax.ppermute(part, "depth", shift_pairs(4, 2))
    ahead, behind, mine, count = pair(False, quarter(1, 3, 0), packed, mix)
    got[1] = lax.ppermute(ahead, "depth", shift_pairs(4, 1))
    got[3] = lax.ppermute(behind, "depth", shift_pairs(4, 3))

    spots = []
    for p in range(4):
        t = (p + 2 * core - y) & 3
        for h in range(2):
            spots.append(t * 32 + (h ^ core) * 16)
    mine, count = fold(mine, count, got[2])
    pieces = settle(jnp.stack(spots).astype(jnp.int32), mine, count, got[1], got[3])
    landed = lax.all_to_all(
        pieces, "col", 0, 0, axis_index_groups=[[0, 2, 4, 6], [5, 7, 1, 3]], tiled=True
    )
    given = flip(landed[2:4])
    return lay((core * RES).astype(jnp.int32).reshape(1), landed[0:2], given)


def solution(mesh):
    return jax.shard_map(
        per_device,
        mesh=mesh,
        in_specs=(
            P("depth", ("row", "col"), None),
            P("depth", ("row", "col")),
            P(),
            P(),
            P(),
            P(),
            P(),
            P(),
            P(),
        ),
        out_specs=P(("row", "depth"), "col", None),
        check_vma=False,
    )
```

```python
import functools

import jax
import jax.numpy as jnp
from jax import lax
from jax.experimental import pallas as pl
from jax.experimental.pallas import tpu as pltpu
from jax.sharding import PartitionSpec as P

F32 = jnp.float32
BF16 = jnp.bfloat16
NT = (((1,), (1,)), ((), ()))
NN = (((1,), (0,)), ((), ()))

SEQ = 256
RES = 16
HID = 32
SHARD = RES * HID
ROWS = SHARD + RES
WIDE = 8 * RES
BIG = 56 * 2**20


def dot(a, b, dims):
    return lax.dot_general(a, b, dims, preferred_element_type=F32)


def project_kernel(sig, mask, gain, shift, w_left, b_left, w_right, b_right, left, right, wide, cols, turn):
    half = sig.shape[0]
    turn[...] = jnp.zeros_like(turn)
    turn[:, 0:HID] = jnp.broadcast_to(b_left[...], (128, HID))
    turn[:, HID : 2 * HID] = jnp.broadcast_to(b_right[...], (128, HID))
    bias = jnp.transpose(turn[...])[0 : 2 * HID, :]
    weights = jnp.concatenate([w_left[...], w_right[...]], axis=0)
    presence = mask[...].astype(F32)

    flat = sig[...].astype(F32).reshape(half * RES, 256)
    wide[0] = flat[:, 0:128]
    wide[1] = flat[:, 128:256]
    for first in range(0, RES, 4):
        normed = []
        for r in range(first, first + 4):
            low = wide[0, pl.ds(r, half, stride=RES), :]
            high = wide[1, pl.ds(r, half, stride=RES), :]
            mean = jnp.sum(low + high, axis=1, keepdims=True) * (1.0 / 256)
            low = low - mean
            high = high - mean
            spread = jnp.sum(low * low + high * high, axis=1, keepdims=True) * (1.0 / 256)
            scale = lax.rsqrt(spread + 1e-5)
            low = low * scale * gain[:, 0:128] + shift[:, 0:128]
            high = high * scale * gain[:, 128:256] + shift[:, 128:256]
            normed.append(jnp.concatenate([low.astype(BF16), high.astype(BF16)], axis=1))
        four = dot(weights, jnp.concatenate(normed, axis=0), NT)
        for r in range(first, first + 4):
            both = (four[:, (r - first) * half : (r - first + 1) * half] + bias) * presence[r : r + 1, :]
            left[r * HID : (r + 1) * HID, :] = both[0:HID].astype(BF16)
            cols[r * HID : (r + 1) * HID, :] = both[HID : 2 * HID]
    for d in range(HID):
        right[d * RES : (d + 1) * RES, :] = cols[pl.ds(d, RES, stride=HID), :].astype(BF16)
    left[SHARD:ROWS, :] = mask[...]
    right[SHARD:ROWS, :] = mask[...]


def project(sig, mask, gain, shift, w_left, b_left, w_right, b_right):
    steps = 2
    half = SEQ // steps
    whole = lambda shape: pl.BlockSpec(shape, lambda s: (0,) * len(shape))
    return pl.pallas_call(
        project_kernel,
        grid=(steps,),
        in_specs=[
            pl.BlockSpec((half, RES, 256), lambda s: (s, 0, 0)),
            pl.BlockSpec((RES, half), lambda s: (0, s)),
            whole((1, 256)),
            whole((1, 256)),
            whole((HID, 256)),
            whole((1, HID)),
            whole((HID, 256)),
            whole((1, HID)),
        ],
        out_specs=[pl.BlockSpec((ROWS, half), lambda s: (0, s))] * 2,
        out_shape=[jax.ShapeDtypeStruct((ROWS, SEQ), BF16)] * 2,
        scratch_shapes=[
            pltpu.VMEM((2, half * RES, 128), F32),
            pltpu.VMEM((SHARD, half), F32),
            pltpu.VMEM((128, 128), F32),
        ],
        compiler_params=pltpu.CompilerParams(vmem_limit_bytes=BIG),
        name="project",
    )(sig, mask, gain, shift, w_left, b_left, w_right, b_right)


def order_kernel(w_out, left_in, right_in, mix, left, right, rows, sorted_rows):
    rows[...] = w_out[...].astype(F32)
    for d in range(HID):
        sorted_rows[d * HID : (d + 1) * HID, :] = rows[pl.ds(d, HID, stride=HID), :]
    for b in range(8):
        mix[:, b * 128 : (b + 1) * 128] = jnp.transpose(sorted_rows[b * 128 : (b + 1) * 128, :]).astype(BF16)
    left[...] = left_in[...]
    right[...] = right_in[...]


def order(w_out, left, right):
    vmem = pl.BlockSpec(memory_space=pltpu.VMEM)
    return pl.pallas_call(
        order_kernel,
        in_specs=[vmem] * 3,
        out_specs=[vmem] * 3,
        out_shape=[jax.ShapeDtypeStruct((128, HID * HID), BF16)] + [jax.ShapeDtypeStruct((ROWS, SEQ), BF16)] * 2,
        scratch_shapes=[pltpu.VMEM((HID * HID, 128), F32)] * 2,
        compiler_params=pltpu.CompilerParams(vmem_limit_bytes=8 * 2**20),
        name="order",
    )(w_out, left, right)


def choose_kernel(which, a, b, out):
    @pl.when(which[0] == 0)
    def _():
        out[...] = a[...]

    @pl.when(which[0] != 0)
    def _():
        out[...] = b[...]


def choose(which, a, b):
    vmem = pl.BlockSpec(memory_space=pltpu.VMEM)
    return pl.pallas_call(
        choose_kernel,
        in_specs=[pl.BlockSpec(memory_space=pltpu.SMEM)] + [vmem] * 2,
        out_specs=vmem,
        out_shape=jax.ShapeDtypeStruct(a.shape, a.dtype),
        compiler_params=pltpu.CompilerParams(vmem_limit_bytes=4 * 2**20),
        name="choose",
    )(which, a, b)


def pair_kernel(first, place, *refs):
    if first:
        lefts, rights, mix, out, packed, outer = refs[0:4], refs[4:12], *refs[12:]
        for t in range(4):
            packed[t] = lefts[t][...]
        for v in range(8):
            packed[4 + v] = rights[v][...]
        outs = [out]
    else:
        packed, mix, *outs, own, count, outer = refs

    def right(v, rows):
        return rights[v][rows, :] if first else packed[4 + v, rows, :]

    weights = jnp.concatenate([right(v, slice(SHARD, ROWS)) for v in range(8)], axis=0)
    for q in range(1 if first else 3):
        which = place[q]
        rows = packed[which, 0:SHARD, :]
        for step in range(HID // 2):
            parts = []
            for dd in range(2):
                start = (step * 2 + dd) * RES
                parts += [right(v, slice(start, start + RES)) for v in range(8)]
            prod = dot(rows, jnp.concatenate(parts, axis=0), NT).astype(BF16)
            for dd in range(2):
                at = (step * 2 + dd) * HID
                for i in range(RES):
                    outer[i // 2, at : at + HID, (i % 2) * 128 : (i % 2) * 128 + 128] = prod[
                        i * HID : (i + 1) * HID, dd * 128 : (dd + 1) * 128
                    ]
        for pair in range(RES // 2):
            mixed = dot(mix[...], outer[pair], NN)
            for ii in range(2):
                at = (pair * 2 + ii) * WIDE
                turned = jnp.transpose(mixed[:, ii * 128 : (ii + 1) * 128])
                if q < len(outs):
                    outs[q][at : at + WIDE, :] = turned.astype(BF16)
                else:
                    own[at : at + WIDE, :] = turned
        tally = dot(packed[which, SHARD:ROWS, :], weights, NT)
        if q < len(outs):
            high = tally.astype(BF16)
            outs[q][RES * WIDE : RES * WIDE + RES, :] = high
            outs[q][RES * WIDE + RES : RES * WIDE + 2 * RES, :] = (tally - high.astype(F32)).astype(BF16)
        else:
            count[...] = tally


def pair(first, place, *args):
    vmem = pl.BlockSpec(memory_space=pltpu.VMEM)
    part = jax.ShapeDtypeStruct((RES * WIDE + 2 * RES, 128), BF16)
    if first:
        out_shape = [part, jax.ShapeDtypeStruct((12, ROWS, SEQ), BF16)]
    else:
        out_shape = [
            part,
            part,
            jax.ShapeDtypeStruct((RES * WIDE, 128), F32),
            jax.ShapeDtypeStruct((RES, 128), F32),
        ]
    return pl.pallas_call(
        functools.partial(pair_kernel, first),
        in_specs=[pl.BlockSpec(memory_space=pltpu.SMEM)] + [vmem] * len(args),
        out_specs=[vmem] * len(out_shape),
        out_shape=out_shape,
        scratch_shapes=[pltpu.VMEM((RES // 2, HID * HID, 256), BF16)],
        compiler_params=pltpu.CompilerParams(vmem_limit_bytes=12 * 2**20),
        cost_estimate=pl.CostEstimate(flops=2**28, bytes_accessed=2**16, transcendentals=0),
        name="pair_first" if first else "pair_rest",
    )(place, *args)


def fold_kernel(mine, count, part, total, total_count):
    end = RES * WIDE
    total[...] = mine[...] + part[0:end, :].astype(F32)
    high, low = part[end : end + RES, :].astype(F32), part[end + RES : end + 2 * RES, :].astype(F32)
    total_count[...] = count[...] + (high + low)


def fold(mine, count, part):
    vmem = pl.BlockSpec(memory_space=pltpu.VMEM)
    return pl.pallas_call(
        fold_kernel,
        in_specs=[vmem] * 3,
        out_specs=[vmem] * 2,
        out_shape=[jax.ShapeDtypeStruct(mine.shape, F32), jax.ShapeDtypeStruct(count.shape, F32)],
        compiler_params=pltpu.CompilerParams(vmem_limit_bytes=8 * 2**20),
        name="fold",
    )(mine, count, part)


def settle_kernel(place, mine, count, a, b, pieces, inverse):
    end = RES * WIDE
    total = count[...]
    for ref in (a, b):
        total = total + (ref[end : end + RES, :].astype(F32) + ref[end + RES : end + 2 * RES, :].astype(F32))
    inverse[0:RES, :] = 1.0 / jnp.maximum(total, 1.0)
    inverse[...] = jnp.transpose(inverse[...])
    for p in range(4):
        for h in range(2):
            start = pl.multiple_of(place[p * 2 + h], RES)
            factor = inverse[pl.ds(start, RES), :]
            for i in range(RES):
                rows = pl.ds(pl.multiple_of(start + i * WIDE, RES), RES)
                value = mine[rows, :] + (a[rows, :].astype(F32) + b[rows, :].astype(F32))
                pieces[p, i, h * RES : (h + 1) * RES, :] = (value * factor[:, i : i + 1]).astype(BF16)


def settle(place, mine, count, a, b):
    vmem = pl.BlockSpec(memory_space=pltpu.VMEM)
    return pl.pallas_call(
        settle_kernel,
        in_specs=[pl.BlockSpec(memory_space=pltpu.SMEM)] + [vmem] * 4,
        out_specs=vmem,
        out_shape=jax.ShapeDtypeStruct((4, RES, 2 * RES, 128), BF16),
        scratch_shapes=[pltpu.VMEM((128, 128), F32)],
        compiler_params=pltpu.CompilerParams(vmem_limit_bytes=8 * 2**20),
        name="settle",
    )(place, mine, count, a, b)


def lay_kernel(place, kept, given, out):
    mine = pl.ds(pl.multiple_of(place[0], RES), RES)
    theirs = pl.ds(pl.multiple_of(RES - place[0], RES), RES)
    for half in range(2):
        span = slice(half * 2 * RES, (half + 1) * 2 * RES)
        out[mine, span, :] = kept[half]
        out[theirs, span, :] = given[half]


def lay(place, kept, given):
    vmem = pl.BlockSpec(memory_space=pltpu.VMEM)
    return pl.pallas_call(
        lay_kernel,
        in_specs=[pl.BlockSpec(memory_space=pltpu.SMEM)] + [vmem] * 2,
        out_specs=vmem,
        out_shape=jax.ShapeDtypeStruct((2 * RES, 4 * RES, 128), BF16),
        compiler_params=pltpu.CompilerParams(vmem_limit_bytes=8 * 2**20),
        name="lay",
    )(place, kept, given)


def shift_pairs(n, step):
    return [(s, (s + step) % n) for s in range(n)]


def per_device(sig, mask, gain, shift, w_left, b_left, w_right, b_right, w_out):
    x = lax.axis_index("depth")
    y = lax.axis_index("row")
    col = lax.axis_index("col")
    z, core = col >> 1, col & 1

    left, right = project(
        sig,
        mask.T,
        gain.reshape(1, 256),
        shift.reshape(1, 256),
        w_left.T,
        b_left.reshape(1, HID),
        w_right.T,
        b_right.reshape(1, HID),
    )

    flip = lambda v: lax.ppermute(v, "col", [(s, s ^ 1) for s in range(8)])
    rights = {0: right}
    lefts = {0: left}
    for t in (1, 3):
        lefts[t] = lax.ppermute(left, "col", shift_pairs(8, -2 * t))
        rights[t] = lax.ppermute(right, "row", shift_pairs(4, -t))
    def relay(near, axis):
        pairs = []
        for sy in range(4):
            for sz in range(4):
                for sc in range(2):
                    step = 2 * sc - 1
                    dy, dz = ((sy + step) % 4, sz) if axis == "row" else (sy, (sz + step) % 4)
                    pairs.append((8 * sy + 2 * sz + sc, 8 * dy + 2 * dz + sc))
        return lax.ppermute(near, ("row", "col"), pairs)

    which = core.astype(jnp.int32).reshape(1)
    rights[2] = relay(choose(which, rights[1], rights[3]), "row")
    passed = choose(which, lefts[1], lefts[3])
    own, rights[1], rights[3], passed = lax.optimization_barrier((right, rights[1], rights[3], passed))
    lefts[2] = relay(passed, "col")
    late_left, late_right, rights[2] = lax.optimization_barrier((left, right, rights[2]))
    mix, lefts[0], rights[0] = order(w_out, late_left, late_right)
    columns = []
    for t in range(4):
        columns += [rights[t], flip(rights[t] if t else own)]
    rows = [lefts[t] for t in range(4)]

    quarter = lambda *ks: jnp.stack([(x + k - z) & 3 for k in ks]).astype(jnp.int32)
    got = {}
    part, packed = pair(True, quarter(2), *rows, *columns, mix)
    got[2] = lax.ppermute(part, "depth", shift_pairs(4, 2))
    ahead, behind, mine, count = pair(False, quarter(1, 3, 0), packed, mix)
    got[1] = lax.ppermute(ahead, "depth", shift_pairs(4, 1))
    got[3] = lax.ppermute(behind, "depth", shift_pairs(4, 3))

    spots = []
    for p in range(4):
        t = (p + 2 * core - y) & 3
        for h in range(2):
            spots.append(t * 32 + (h ^ core) * 16)
    mine, count = fold(mine, count, got[2])
    pieces = settle(jnp.stack(spots).astype(jnp.int32), mine, count, got[1], got[3])
    landed = lax.all_to_all(
        pieces, "col", 0, 0, axis_index_groups=[[0, 2, 4, 6], [5, 7, 1, 3]], tiled=True
    )
    given = flip(landed[2:4])
    return lay((core * RES).astype(jnp.int32).reshape(1), landed[0:2], given)


def solution(mesh):
    return jax.shard_map(
        per_device,
        mesh=mesh,
        in_specs=(
            P("depth", ("row", "col"), None),
            P("depth", ("row", "col")),
            P(),
            P(),
            P(),
            P(),
            P(),
            P(),
            P(),
        ),
        out_specs=P(("row", "depth"), "col", None),
        check_vma=False,
    )
```

```python
import functools

import jax
import jax.numpy as jnp
from jax import lax
from jax.experimental import pallas as pl
from jax.experimental.pallas import tpu as pltpu
from jax.sharding import PartitionSpec as P

F32 = jnp.float32
BF16 = jnp.bfloat16
NT = (((1,), (1,)), ((), ()))
NN = (((1,), (0,)), ((), ()))

SEQ = 256
RES = 16
HID = 32
SHARD = RES * HID
ROWS = SHARD + RES
WIDE = 8 * RES
BIG = 62 * 2**20


def dot(a, b, dims):
    return lax.dot_general(a, b, dims, preferred_element_type=F32)


def project_kernel(sig, mask, gain, shift, w_left, b_left, w_right, b_right, left, right, wide, cols, turn):
    half = sig.shape[0]
    turn[...] = jnp.zeros_like(turn)
    turn[:, 0:HID] = jnp.broadcast_to(b_left[...], (128, HID))
    turn[:, HID : 2 * HID] = jnp.broadcast_to(b_right[...], (128, HID))
    bias = jnp.transpose(turn[...])[0 : 2 * HID, :]
    weights = jnp.concatenate([w_left[...], w_right[...]], axis=0)
    presence = mask[...].astype(F32)

    flat = sig[...].astype(F32).reshape(half * RES, 256)
    wide[0] = flat[:, 0:128]
    wide[1] = flat[:, 128:256]
    for first in range(0, RES, 4):
        normed = []
        for r in range(first, first + 4):
            low = wide[0, pl.ds(r, half, stride=RES), :]
            high = wide[1, pl.ds(r, half, stride=RES), :]
            mean = jnp.sum(low + high, axis=1, keepdims=True) * (1.0 / 256)
            low = low - mean
            high = high - mean
            spread = jnp.sum(low * low + high * high, axis=1, keepdims=True) * (1.0 / 256)
            scale = lax.rsqrt(spread + 1e-5)
            low = low * scale * gain[:, 0:128] + shift[:, 0:128]
            high = high * scale * gain[:, 128:256] + shift[:, 128:256]
            normed.append(jnp.concatenate([low.astype(BF16), high.astype(BF16)], axis=1))
        four = dot(weights, jnp.concatenate(normed, axis=0), NT)
        for r in range(first, first + 4):
            both = (four[:, (r - first) * half : (r - first + 1) * half] + bias) * presence[r : r + 1, :]
            left[r * HID : (r + 1) * HID, :] = both[0:HID].astype(BF16)
            cols[r * HID : (r + 1) * HID, :] = both[HID : 2 * HID]
    for d in range(HID):
        right[d * RES : (d + 1) * RES, :] = cols[pl.ds(d, RES, stride=HID), :].astype(BF16)
    left[SHARD:ROWS, :] = mask[...]
    right[SHARD:ROWS, :] = mask[...]


def project(sig, mask, gain, shift, w_left, b_left, w_right, b_right):
    steps = 2
    half = SEQ // steps
    whole = lambda shape: pl.BlockSpec(shape, lambda s: (0,) * len(shape))
    return pl.pallas_call(
        project_kernel,
        grid=(steps,),
        in_specs=[
            pl.BlockSpec((half, RES, 256), lambda s: (s, 0, 0)),
            pl.BlockSpec((RES, half), lambda s: (0, s)),
            whole((1, 256)),
            whole((1, 256)),
            whole((HID, 256)),
            whole((1, HID)),
            whole((HID, 256)),
            whole((1, HID)),
        ],
        out_specs=[pl.BlockSpec((ROWS, half), lambda s: (0, s))] * 2,
        out_shape=[jax.ShapeDtypeStruct((ROWS, SEQ), BF16)] * 2,
        scratch_shapes=[
            pltpu.VMEM((2, half * RES, 128), F32),
            pltpu.VMEM((SHARD, half), F32),
            pltpu.VMEM((128, 128), F32),
        ],
        compiler_params=pltpu.CompilerParams(vmem_limit_bytes=BIG),
        name="project",
    )(sig, mask, gain, shift, w_left, b_left, w_right, b_right)


def order_kernel(w_out, left_in, right_in, mix, left, right, rows, sorted_rows):
    rows[...] = w_out[...].astype(F32)
    for d in range(HID):
        sorted_rows[d * HID : (d + 1) * HID, :] = rows[pl.ds(d, HID, stride=HID), :]
    for b in range(8):
        mix[:, b * 128 : (b + 1) * 128] = jnp.transpose(sorted_rows[b * 128 : (b + 1) * 128, :]).astype(BF16)
    left[...] = left_in[...]
    right[...] = right_in[...]


def order(w_out, left, right):
    vmem = pl.BlockSpec(memory_space=pltpu.VMEM)
    return pl.pallas_call(
        order_kernel,
        in_specs=[vmem] * 3,
        out_specs=[vmem] * 3,
        out_shape=[jax.ShapeDtypeStruct((128, HID * HID), BF16)] + [jax.ShapeDtypeStruct((ROWS, SEQ), BF16)] * 2,
        scratch_shapes=[pltpu.VMEM((HID * HID, 128), F32)] * 2,
        compiler_params=pltpu.CompilerParams(vmem_limit_bytes=8 * 2**20),
        name="order",
    )(w_out, left, right)


def choose_kernel(which, a, b, out):
    @pl.when(which[0] == 0)
    def _():
        out[...] = a[...]

    @pl.when(which[0] != 0)
    def _():
        out[...] = b[...]


def choose(which, a, b):
    vmem = pl.BlockSpec(memory_space=pltpu.VMEM)
    return pl.pallas_call(
        choose_kernel,
        in_specs=[pl.BlockSpec(memory_space=pltpu.SMEM)] + [vmem] * 2,
        out_specs=vmem,
        out_shape=jax.ShapeDtypeStruct(a.shape, a.dtype),
        compiler_params=pltpu.CompilerParams(vmem_limit_bytes=4 * 2**20),
        name="choose",
    )(which, a, b)


def pair_kernel(first, place, *refs):
    if first:
        lefts, rights, mix, out, packed, outer = refs[0:4], refs[4:12], *refs[12:]
        for t in range(4):
            packed[t] = lefts[t][...]
        for v in range(8):
            packed[4 + v] = rights[v][...]
        outs = [out]
    else:
        packed, mix, *outs, own, count, outer = refs

    def right(v, rows):
        return rights[v][rows, :] if first else packed[4 + v, rows, :]

    weights = jnp.concatenate([right(v, slice(SHARD, ROWS)) for v in range(8)], axis=0)
    for q in range(1 if first else 3):
        which = place[q]
        rows = packed[which, 0:SHARD, :]
        for step in range(HID // 2):
            parts = []
            for dd in range(2):
                start = (step * 2 + dd) * RES
                parts += [right(v, slice(start, start + RES)) for v in range(8)]
            prod = dot(rows, jnp.concatenate(parts, axis=0), NT).astype(BF16)
            for dd in range(2):
                at = (step * 2 + dd) * HID
                for i in range(RES):
                    outer[i // 2, at : at + HID, (i % 2) * 128 : (i % 2) * 128 + 128] = prod[
                        i * HID : (i + 1) * HID, dd * 128 : (dd + 1) * 128
                    ]
        for pair in range(RES // 2):
            mixed = dot(mix[...], outer[pair], NN)
            for ii in range(2):
                at = (pair * 2 + ii) * WIDE
                turned = jnp.transpose(mixed[:, ii * 128 : (ii + 1) * 128])
                if q < len(outs):
                    outs[q][at : at + WIDE, :] = turned.astype(BF16)
                else:
                    own[at : at + WIDE, :] = turned
        tally = dot(packed[which, SHARD:ROWS, :], weights, NT)
        if q < len(outs):
            high = tally.astype(BF16)
            outs[q][RES * WIDE : RES * WIDE + RES, :] = high
            outs[q][RES * WIDE + RES : RES * WIDE + 2 * RES, :] = (tally - high.astype(F32)).astype(BF16)
        else:
            count[...] = tally


def pair(first, place, *args):
    vmem = pl.BlockSpec(memory_space=pltpu.VMEM)
    part = jax.ShapeDtypeStruct((RES * WIDE + 2 * RES, 128), BF16)
    if first:
        out_shape = [part, jax.ShapeDtypeStruct((12, ROWS, SEQ), BF16)]
    else:
        out_shape = [
            part,
            part,
            jax.ShapeDtypeStruct((RES * WIDE, 128), F32),
            jax.ShapeDtypeStruct((RES, 128), F32),
        ]
    return pl.pallas_call(
        functools.partial(pair_kernel, first),
        in_specs=[pl.BlockSpec(memory_space=pltpu.SMEM)] + [vmem] * len(args),
        out_specs=[vmem] * len(out_shape),
        out_shape=out_shape,
        scratch_shapes=[pltpu.VMEM((RES // 2, HID * HID, 256), BF16)],
        compiler_params=pltpu.CompilerParams(vmem_limit_bytes=12 * 2**20),
        cost_estimate=pl.CostEstimate(flops=2**28, bytes_accessed=2**16, transcendentals=0),
        name="pair_first" if first else "pair_rest",
    )(place, *args)


def fold_kernel(mine, count, part, total, total_count):
    end = RES * WIDE
    total[...] = mine[...] + part[0:end, :].astype(F32)
    high, low = part[end : end + RES, :].astype(F32), part[end + RES : end + 2 * RES, :].astype(F32)
    total_count[...] = count[...] + (high + low)


def fold(mine, count, part):
    vmem = pl.BlockSpec(memory_space=pltpu.VMEM)
    return pl.pallas_call(
        fold_kernel,
        in_specs=[vmem] * 3,
        out_specs=[vmem] * 2,
        out_shape=[jax.ShapeDtypeStruct(mine.shape, F32), jax.ShapeDtypeStruct(count.shape, F32)],
        compiler_params=pltpu.CompilerParams(vmem_limit_bytes=8 * 2**20),
        name="fold",
    )(mine, count, part)


def settle_kernel(place, mine, count, a, b, pieces, inverse):
    end = RES * WIDE
    total = count[...]
    for ref in (a, b):
        total = total + (ref[end : end + RES, :].astype(F32) + ref[end + RES : end + 2 * RES, :].astype(F32))
    inverse[0:RES, :] = 1.0 / jnp.maximum(total, 1.0)
    inverse[...] = jnp.transpose(inverse[...])
    for p in range(4):
        for h in range(2):
            start = pl.multiple_of(place[p * 2 + h], RES)
            factor = inverse[pl.ds(start, RES), :]
            for i in range(RES):
                rows = pl.ds(pl.multiple_of(start + i * WIDE, RES), RES)
                value = mine[rows, :] + (a[rows, :].astype(F32) + b[rows, :].astype(F32))
                pieces[p, i, h * RES : (h + 1) * RES, :] = (value * factor[:, i : i + 1]).astype(BF16)


def settle(place, mine, count, a, b):
    vmem = pl.BlockSpec(memory_space=pltpu.VMEM)
    return pl.pallas_call(
        settle_kernel,
        in_specs=[pl.BlockSpec(memory_space=pltpu.SMEM)] + [vmem] * 4,
        out_specs=vmem,
        out_shape=jax.ShapeDtypeStruct((4, RES, 2 * RES, 128), BF16),
        scratch_shapes=[pltpu.VMEM((128, 128), F32)],
        compiler_params=pltpu.CompilerParams(vmem_limit_bytes=8 * 2**20),
        name="settle",
    )(place, mine, count, a, b)


def lay_kernel(place, kept, given, out):
    mine = pl.ds(pl.multiple_of(place[0], RES), RES)
    theirs = pl.ds(pl.multiple_of(RES - place[0], RES), RES)
    for half in range(2):
        span = slice(half * 2 * RES, (half + 1) * 2 * RES)
        out[mine, span, :] = kept[half]
        out[theirs, span, :] = given[half]


def lay(place, kept, given):
    vmem = pl.BlockSpec(memory_space=pltpu.VMEM)
    return pl.pallas_call(
        lay_kernel,
        in_specs=[pl.BlockSpec(memory_space=pltpu.SMEM)] + [vmem] * 2,
        out_specs=vmem,
        out_shape=jax.ShapeDtypeStruct((2 * RES, 4 * RES, 128), BF16),
        compiler_params=pltpu.CompilerParams(vmem_limit_bytes=8 * 2**20),
        name="lay",
    )(place, kept, given)


def shift_pairs(n, step):
    return [(s, (s + step) % n) for s in range(n)]


def per_device(sig, mask, gain, shift, w_left, b_left, w_right, b_right, w_out):
    x = lax.axis_index("depth")
    y = lax.axis_index("row")
    col = lax.axis_index("col")
    z, core = col >> 1, col & 1

    left, right = project(
        sig,
        mask.T,
        gain.reshape(1, 256),
        shift.reshape(1, 256),
        w_left.T,
        b_left.reshape(1, HID),
        w_right.T,
        b_right.reshape(1, HID),
    )

    flip = lambda v: lax.ppermute(v, "col", [(s, s ^ 1) for s in range(8)])
    rights = {0: right}
    lefts = {0: left}
    for t in (1, 3):
        lefts[t] = lax.ppermute(left, "col", shift_pairs(8, -2 * t))
        rights[t] = lax.ppermute(right, "row", shift_pairs(4, -t))
    def relay(near, axis):
        pairs = []
        for sy in range(4):
            for sz in range(4):
                for sc in range(2):
                    step = 2 * sc - 1
                    dy, dz = ((sy + step) % 4, sz) if axis == "row" else (sy, (sz + step) % 4)
                    pairs.append((8 * sy + 2 * sz + sc, 8 * dy + 2 * dz + sc))
        return lax.ppermute(near, ("row", "col"), pairs)

    which = core.astype(jnp.int32).reshape(1)
    rights[2] = relay(choose(which, rights[1], rights[3]), "row")
    passed = choose(which, lefts[1], lefts[3])
    own, rights[1], rights[3], passed = lax.optimization_barrier((right, rights[1], rights[3], passed))
    lefts[2] = relay(passed, "col")
    late_left, late_right, rights[2] = lax.optimization_barrier((left, right, rights[2]))
    mix, lefts[0], rights[0] = order(w_out, late_left, late_right)
    columns = []
    for t in range(4):
        columns += [rights[t], flip(rights[t] if t else own)]
    rows = [lefts[t] for t in range(4)]

    quarter = lambda *ks: jnp.stack([(x + k - z) & 3 for k in ks]).astype(jnp.int32)
    got = {}
    part, packed = pair(True, quarter(2), *rows, *columns, mix)
    got[2] = lax.ppermute(part, "depth", shift_pairs(4, 2))
    ahead, behind, mine, count = pair(False, quarter(1, 3, 0), packed, mix)
    got[1] = lax.ppermute(ahead, "depth", shift_pairs(4, 1))
    got[3] = lax.ppermute(behind, "depth", shift_pairs(4, 3))

    spots = []
    for p in range(4):
        t = (p + 2 * core - y) & 3
        for h in range(2):
            spots.append(t * 32 + (h ^ core) * 16)
    mine, count = fold(mine, count, got[2])
    pieces = settle(jnp.stack(spots).astype(jnp.int32), mine, count, got[1], got[3])
    landed = lax.all_to_all(
        pieces, "col", 0, 0, axis_index_groups=[[0, 2, 4, 6], [5, 7, 1, 3]], tiled=True
    )
    given = flip(landed[2:4])
    return lay((core * RES).astype(jnp.int32).reshape(1), landed[0:2], given)


def solution(mesh):
    return jax.shard_map(
        per_device,
        mesh=mesh,
        in_specs=(
            P("depth", ("row", "col"), None),
            P("depth", ("row", "col")),
            P(),
            P(),
            P(),
            P(),
            P(),
            P(),
            P(),
        ),
        out_specs=P(("row", "depth"), "col", None),
        check_vma=False,
    )
```

```python
import functools

import jax
import jax.numpy as jnp
from jax import lax
from jax.experimental import pallas as pl
from jax.experimental.pallas import tpu as pltpu
from jax.sharding import PartitionSpec as P

F32 = jnp.float32
BF16 = jnp.bfloat16
NT = (((1,), (1,)), ((), ()))
NN = (((1,), (0,)), ((), ()))

SEQ = 256
RES = 16
HID = 32
SHARD = RES * HID
ROWS = SHARD + RES
WIDE = 8 * RES
BIG = 62 * 2**20


def dot(a, b, dims):
    return lax.dot_general(a, b, dims, preferred_element_type=F32)


def project_kernel(sig, mask, gain, shift, w_left, b_left, w_right, b_right, left, right, wide, cols, turn):
    half = sig.shape[0]
    turn[...] = jnp.zeros_like(turn)
    turn[:, 0:HID] = jnp.broadcast_to(b_left[...], (128, HID))
    turn[:, HID : 2 * HID] = jnp.broadcast_to(b_right[...], (128, HID))
    bias = jnp.transpose(turn[...])[0 : 2 * HID, :]
    weights = jnp.concatenate([w_left[...], w_right[...]], axis=0)
    presence = mask[...].astype(F32)

    flat = sig[...].astype(F32).reshape(half * RES, 256)
    wide[0] = flat[:, 0:128]
    wide[1] = flat[:, 128:256]
    for first in range(0, RES, 4):
        normed = []
        for r in range(first, first + 4):
            low = wide[0, pl.ds(r, half, stride=RES), :]
            high = wide[1, pl.ds(r, half, stride=RES), :]
            mean = jnp.sum(low + high, axis=1, keepdims=True) * (1.0 / 256)
            low = low - mean
            high = high - mean
            spread = jnp.sum(low * low + high * high, axis=1, keepdims=True) * (1.0 / 256)
            scale = lax.rsqrt(spread + 1e-5)
            low = low * scale * gain[:, 0:128] + shift[:, 0:128]
            high = high * scale * gain[:, 128:256] + shift[:, 128:256]
            normed.append(jnp.concatenate([low.astype(BF16), high.astype(BF16)], axis=1))
        four = dot(weights, jnp.concatenate(normed, axis=0), NT)
        for r in range(first, first + 4):
            both = (four[:, (r - first) * half : (r - first + 1) * half] + bias) * presence[r : r + 1, :]
            left[r * HID : (r + 1) * HID, :] = both[0:HID].astype(BF16)
            cols[r * HID : (r + 1) * HID, :] = both[HID : 2 * HID]
    for d in range(HID):
        right[d * RES : (d + 1) * RES, :] = cols[pl.ds(d, RES, stride=HID), :].astype(BF16)
    left[SHARD:ROWS, :] = mask[...]
    right[SHARD:ROWS, :] = mask[...]


def project(sig, mask, gain, shift, w_left, b_left, w_right, b_right):
    steps = 2
    half = SEQ // steps
    whole = lambda shape: pl.BlockSpec(shape, lambda s: (0,) * len(shape))
    return pl.pallas_call(
        project_kernel,
        grid=(steps,),
        in_specs=[
            pl.BlockSpec((half, RES, 256), lambda s: (s, 0, 0)),
            pl.BlockSpec((RES, half), lambda s: (0, s)),
            whole((1, 256)),
            whole((1, 256)),
            whole((HID, 256)),
            whole((1, HID)),
            whole((HID, 256)),
            whole((1, HID)),
        ],
        out_specs=[pl.BlockSpec((ROWS, half), lambda s: (0, s))] * 2,
        out_shape=[jax.ShapeDtypeStruct((ROWS, SEQ), BF16)] * 2,
        scratch_shapes=[
            pltpu.VMEM((2, half * RES, 128), F32),
            pltpu.VMEM((SHARD, half), F32),
            pltpu.VMEM((128, 128), F32),
        ],
        compiler_params=pltpu.CompilerParams(vmem_limit_bytes=BIG),
        name="project",
    )(sig, mask, gain, shift, w_left, b_left, w_right, b_right)


def order_kernel(w_out, left_in, right_in, mix, left, right, rows, sorted_rows):
    rows[...] = w_out[...].astype(F32)
    for d in range(HID):
        sorted_rows[d * HID : (d + 1) * HID, :] = rows[pl.ds(d, HID, stride=HID), :]
    for b in range(8):
        mix[:, b * 128 : (b + 1) * 128] = jnp.transpose(sorted_rows[b * 128 : (b + 1) * 128, :]).astype(BF16)
    left[...] = left_in[...]
    right[...] = right_in[...]


def order(w_out, left, right):
    vmem = pl.BlockSpec(memory_space=pltpu.VMEM)
    return pl.pallas_call(
        order_kernel,
        in_specs=[vmem] * 3,
        out_specs=[vmem] * 3,
        out_shape=[jax.ShapeDtypeStruct((128, HID * HID), BF16)] + [jax.ShapeDtypeStruct((ROWS, SEQ), BF16)] * 2,
        scratch_shapes=[pltpu.VMEM((HID * HID, 128), F32)] * 2,
        compiler_params=pltpu.CompilerParams(vmem_limit_bytes=8 * 2**20),
        name="order",
    )(w_out, left, right)


def choose_kernel(which, a, b, out):
    @pl.when(which[0] == 0)
    def _():
        out[...] = a[...]

    @pl.when(which[0] != 0)
    def _():
        out[...] = b[...]


def choose(which, a, b):
    vmem = pl.BlockSpec(memory_space=pltpu.VMEM)
    return pl.pallas_call(
        choose_kernel,
        in_specs=[pl.BlockSpec(memory_space=pltpu.SMEM)] + [vmem] * 2,
        out_specs=vmem,
        out_shape=jax.ShapeDtypeStruct(a.shape, a.dtype),
        compiler_params=pltpu.CompilerParams(vmem_limit_bytes=4 * 2**20),
        name="choose",
    )(which, a, b)


def pair_kernel(first, place, *refs):
    if first:
        lefts, rights, mix, out, packed, outer = refs[0:4], refs[4:12], *refs[12:]
        for t in range(4):
            packed[t] = lefts[t][...]
        for v in range(8):
            packed[4 + v] = rights[v][...]
        outs = [out]
    else:
        packed, mix, *outs, own, count, outer = refs

    def right(v, rows):
        return rights[v][rows, :] if first else packed[4 + v, rows, :]

    weights = jnp.concatenate([right(v, slice(SHARD, ROWS)) for v in range(8)], axis=0)
    for q in range(1 if first else 3):
        which = place[q]
        rows = packed[which, 0:SHARD, :]
        for step in range(HID // 2):
            parts = []
            for dd in range(2):
                start = (step * 2 + dd) * RES
                parts += [right(v, slice(start, start + RES)) for v in range(8)]
            prod = dot(rows, jnp.concatenate(parts, axis=0), NT).astype(BF16)
            for dd in range(2):
                at = (step * 2 + dd) * HID
                for i in range(RES):
                    outer[i // 2, at : at + HID, (i % 2) * 128 : (i % 2) * 128 + 128] = prod[
                        i * HID : (i + 1) * HID, dd * 128 : (dd + 1) * 128
                    ]
        for pair in range(RES // 2):
            mixed = dot(mix[...], outer[pair], NN)
            for ii in range(2):
                at = (pair * 2 + ii) * WIDE
                turned = jnp.transpose(mixed[:, ii * 128 : (ii + 1) * 128])
                if q < len(outs):
                    outs[q][at : at + WIDE, :] = turned.astype(BF16)
                else:
                    own[at : at + WIDE, :] = turned
        tally = dot(packed[which, SHARD:ROWS, :], weights, NT)
        if q < len(outs):
            high = tally.astype(BF16)
            outs[q][RES * WIDE : RES * WIDE + RES, :] = high
            outs[q][RES * WIDE + RES : RES * WIDE + 2 * RES, :] = (tally - high.astype(F32)).astype(BF16)
        else:
            count[...] = tally


def pair(first, place, *args):
    vmem = pl.BlockSpec(memory_space=pltpu.VMEM)
    part = jax.ShapeDtypeStruct((RES * WIDE + 2 * RES, 128), BF16)
    if first:
        out_shape = [part, jax.ShapeDtypeStruct((12, ROWS, SEQ), BF16)]
    else:
        out_shape = [
            part,
            part,
            jax.ShapeDtypeStruct((RES * WIDE, 128), F32),
            jax.ShapeDtypeStruct((RES, 128), F32),
        ]
    return pl.pallas_call(
        functools.partial(pair_kernel, first),
        in_specs=[pl.BlockSpec(memory_space=pltpu.SMEM)] + [vmem] * len(args),
        out_specs=[vmem] * len(out_shape),
        out_shape=out_shape,
        scratch_shapes=[pltpu.VMEM((RES // 2, HID * HID, 256), BF16)],
        compiler_params=pltpu.CompilerParams(vmem_limit_bytes=12 * 2**20),
        cost_estimate=pl.CostEstimate(flops=2**28, bytes_accessed=2**16, transcendentals=0),
        name="pair_first" if first else "pair_rest",
    )(place, *args)


def fold_kernel(mine, count, part, total, total_count):
    end = RES * WIDE
    total[...] = mine[...] + part[0:end, :].astype(F32)
    high, low = part[end : end + RES, :].astype(F32), part[end + RES : end + 2 * RES, :].astype(F32)
    total_count[...] = count[...] + (high + low)


def fold(mine, count, part):
    vmem = pl.BlockSpec(memory_space=pltpu.VMEM)
    return pl.pallas_call(
        fold_kernel,
        in_specs=[vmem] * 3,
        out_specs=[vmem] * 2,
        out_shape=[jax.ShapeDtypeStruct(mine.shape, F32), jax.ShapeDtypeStruct(count.shape, F32)],
        compiler_params=pltpu.CompilerParams(vmem_limit_bytes=8 * 2**20),
        name="fold",
    )(mine, count, part)


def settle_kernel(place, mine, count, a, b, pieces, inverse):
    end = RES * WIDE
    total = count[...]
    for ref in (a, b):
        total = total + (ref[end : end + RES, :].astype(F32) + ref[end + RES : end + 2 * RES, :].astype(F32))
    inverse[0:RES, :] = 1.0 / jnp.maximum(total, 1.0)
    inverse[...] = jnp.transpose(inverse[...])
    for p in range(4):
        for h in range(2):
            start = pl.multiple_of(place[p * 2 + h], RES)
            factor = inverse[pl.ds(start, RES), :]
            for i in range(RES):
                rows = pl.ds(pl.multiple_of(start + i * WIDE, RES), RES)
                value = mine[rows, :] + (a[rows, :].astype(F32) + b[rows, :].astype(F32))
                pieces[p, i, h * RES : (h + 1) * RES, :] = (value * factor[:, i : i + 1]).astype(BF16)


def settle(place, mine, count, a, b):
    vmem = pl.BlockSpec(memory_space=pltpu.VMEM)
    return pl.pallas_call(
        settle_kernel,
        in_specs=[pl.BlockSpec(memory_space=pltpu.SMEM)] + [vmem] * 4,
        out_specs=vmem,
        out_shape=jax.ShapeDtypeStruct((4, RES, 2 * RES, 128), BF16),
        scratch_shapes=[pltpu.VMEM((128, 128), F32)],
        compiler_params=pltpu.CompilerParams(vmem_limit_bytes=8 * 2**20),
        name="settle",
    )(place, mine, count, a, b)


def lay_kernel(place, kept, given, out):
    mine = pl.ds(pl.multiple_of(place[0], RES), RES)
    theirs = pl.ds(pl.multiple_of(RES - place[0], RES), RES)
    for half in range(2):
        span = slice(half * 2 * RES, (half + 1) * 2 * RES)
        out[mine, span, :] = kept[half]
        out[theirs, span, :] = given[half]


def lay(place, kept, given):
    vmem = pl.BlockSpec(memory_space=pltpu.VMEM)
    return pl.pallas_call(
        lay_kernel,
        in_specs=[pl.BlockSpec(memory_space=pltpu.SMEM)] + [vmem] * 2,
        out_specs=vmem,
        out_shape=jax.ShapeDtypeStruct((2 * RES, 4 * RES, 128), BF16),
        compiler_params=pltpu.CompilerParams(vmem_limit_bytes=8 * 2**20),
        name="lay",
    )(place, kept, given)


def shift_pairs(n, step):
    return [(s, (s + step) % n) for s in range(n)]


def per_device(sig, mask, gain, shift, w_left, b_left, w_right, b_right, w_out):
    x = lax.axis_index("depth")
    y = lax.axis_index("row")
    col = lax.axis_index("col")
    z, core = col >> 1, col & 1

    left, right = project(
        sig,
        mask.T,
        gain.reshape(1, 256),
        shift.reshape(1, 256),
        w_left.T,
        b_left.reshape(1, HID),
        w_right.T,
        b_right.reshape(1, HID),
    )

    flip = lambda v: lax.ppermute(v, "col", [(s, s ^ 1) for s in range(8)])
    rights = {0: right}
    lefts = {0: left}
    for t in (1, 3):
        lefts[t] = lax.ppermute(left, "col", shift_pairs(8, -2 * t))
        rights[t] = lax.ppermute(right, "row", shift_pairs(4, -t))
    def relay(near, axis):
        pairs = []
        for sy in range(4):
            for sz in range(4):
                for sc in range(2):
                    step = 2 * sc - 1
                    dy, dz = ((sy + step) % 4, sz) if axis == "row" else (sy, (sz + step) % 4)
                    pairs.append((8 * sy + 2 * sz + sc, 8 * dy + 2 * dz + sc))
        return lax.ppermute(near, ("row", "col"), pairs)

    which = core.astype(jnp.int32).reshape(1)
    rights[2] = relay(choose(which, rights[1], rights[3]), "row")
    passed = choose(which, lefts[1], lefts[3])
    own, passed = lax.optimization_barrier((right, passed))
    lefts[2] = relay(passed, "col")
    late_left, late_right, rights[2] = lax.optimization_barrier((left, right, rights[2]))
    mix, lefts[0], rights[0] = order(w_out, late_left, late_right)
    columns = []
    for t in range(4):
        columns += [rights[t], flip(rights[t] if t else own)]
    rows = [lefts[t] for t in range(4)]

    quarter = lambda *ks: jnp.stack([(x + k - z) & 3 for k in ks]).astype(jnp.int32)
    got = {}
    part, packed = pair(True, quarter(2), *rows, *columns, mix)
    got[2] = lax.ppermute(part, "depth", shift_pairs(4, 2))
    ahead, behind, mine, count = pair(False, quarter(1, 3, 0), packed, mix)
    got[1] = lax.ppermute(ahead, "depth", shift_pairs(4, 1))
    got[3] = lax.ppermute(behind, "depth", shift_pairs(4, 3))

    spots = []
    for p in range(4):
        t = (p + 2 * core - y) & 3
        for h in range(2):
            spots.append(t * 32 + (h ^ core) * 16)
    mine, count = fold(mine, count, got[2])
    pieces = settle(jnp.stack(spots).astype(jnp.int32), mine, count, got[1], got[3])
    landed = lax.all_to_all(
        pieces, "col", 0, 0, axis_index_groups=[[0, 2, 4, 6], [5, 7, 1, 3]], tiled=True
    )
    given = flip(landed[2:4])
    return lay((core * RES).astype(jnp.int32).reshape(1), landed[0:2], given)


def solution(mesh):
    return jax.shard_map(
        per_device,
        mesh=mesh,
        in_specs=(
            P("depth", ("row", "col"), None),
            P("depth", ("row", "col")),
            P(),
            P(),
            P(),
            P(),
            P(),
            P(),
            P(),
        ),
        out_specs=P(("row", "depth"), "col", None),
        check_vma=False,
    )
```
